32 devices in a mesh: dp: 4 (over x, core), seq: 8 (over z, y).
Axes of the slice: x: 2, y: 2, z: 4, core: 2. Of those that a mesh axis runs over, the one named last changes fastest.
Arguments:
- inputs: bfloat16 [2, 4, 1024, 768], P(None, 'dp', 'seq'), may hold values from -6 to 6
- cotangent: bfloat16 [2, 4, 1024, 768], P(None, 'dp', 'seq'), may hold values from -6 to 6
- live: int32 [2, 4], P(None, 'dp'), may hold values from 0 to 1, as said below
- first_qkv: bfloat16 [768, 2304], P('dp'), may hold values from -1 to 1
- first_out: bfloat16 [768, 768], P('dp'), may hold values from -4 to 4
- first_gain_a: bfloat16 [768], P('dp'), may hold values from 0.099609375 to 1.8984375
- first_shift_a: bfloat16 [768], P('dp'), may hold values from -3 to 3
- first_gate: bfloat16 [768, 3072], P('dp'), may hold values from -0.21875 to 0.21875
- first_up: bfloat16 [768, 3072], P('dp'), may hold values from -0.21875 to 0.21875
- first_down: bfloat16 [3072, 768], P('dp'), may hold values from -0.109375 to 0.109375
- first_gain_f: bfloat16 [768], P('dp'), may hold values from 0.099609375 to 1.8984375
- first_shift_f: bfloat16 [768], P('dp'), may hold values from -3 to 3
- second_qkv: bfloat16 [768, 2304], P('dp'), may hold values from -1 to 1
- second_out: bfloat16 [768, 768], P('dp'), may hold values from -4 to 4
- second_gain_a: bfloat16 [768], P('dp'), may hold values from 0.099609375 to 1.8984375
- second_shift_a: bfloat16 [768], P('dp'), may hold values from -3 to 3
- second_gate: bfloat16 [768, 3072], P('dp'), may hold values from -0.21875 to 0.21875
- second_up: bfloat16 [768, 3072], P('dp'), may hold values from -0.21875 to 0.21875
- second_down: bfloat16 [3072, 768], P('dp'), may hold values from -0.109375 to 0.109375
- second_gain_f: bfloat16 [768], P('dp'), may hold values from 0.099609375 to 1.8984375
- second_shift_f: bfloat16 [768], P('dp'), may hold values from -3 to 3
Outputs:
- output: bfloat16 [2, 4, 1024, 768], P(None, 'dp', 'seq')
- input_grad: bfloat16 [2, 4, 1024, 768], P(None, 'dp', 'seq')
- grad_first_qkv: float32 [768, 2304], P('dp')
- grad_first_out: float32 [768, 768], P('dp')
- grad_first_gain_a: float32 [768], P('dp')
- grad_first_shift_a: float32 [768], P('dp')
- grad_first_gate: float32 [768, 3072], P('dp')
- grad_first_up: float32 [768, 3072], P('dp')
- grad_first_down: float32 [3072, 768], P('dp')
- grad_first_gain_f: float32 [768], P('dp')
- grad_first_shift_f: float32 [768], P('dp')
- grad_second_qkv: float32 [768, 2304], P('dp')
- grad_second_out: float32 [768, 768], P('dp')
- grad_second_gain_a: float32 [768], P('dp')
- grad_second_shift_a: float32 [768], P('dp')
- grad_second_gate: float32 [768, 3072], P('dp')
- grad_second_up: float32 [768, 3072], P('dp')
- grad_second_down: float32 [3072, 768], P('dp')
- grad_second_gain_f: float32 [768], P('dp')
- grad_second_shift_f: float32 [768], P('dp')
The draws below stay inside these ranges and needn't reach their ends.
Inputs may be any that keep to these rules, and one draw needn't show every extreme that they name: One micro-batch, drawn from the seed, has exactly one live slot, also drawn from the seed; every other micro-batch has every slot live.
All inputs are finite; a program needn't handle non-finite values.
Results may differ from the reference program's by a relative error of at most 0.028.
Values may be sent and summed in bfloat16 or wider, within the bound.
A program may use at most 512 MiB of HBM per device.

```python
import jax
import jax.numpy as jnp
from jax import lax

D = 768
HEAD = 64
FF = 3072
MB = 2
SLOTS = 4
LENGTH = 1024


def draw_live(key, part):
    key_batch, key_slot = jax.random.split(jax.random.fold_in(key, 17))
    lone_batch = jax.random.randint(key_batch, (), 0, MB)
    lone_slot = jax.random.randint(key_slot, (), 0, SLOTS)
    batch_ids = jnp.arange(MB)[:, None]
    slot_ids = jnp.arange(SLOTS)[None, :]
    single = (slot_ids == lone_slot).astype(jnp.int32)
    return jnp.where(batch_ids == lone_batch, single, jnp.ones((MB, SLOTS), jnp.int32)).astype(jnp.int32)


def drawn_field(key, shape, scale, bound):
    values = jnp.clip(jax.random.normal(key, shape, jnp.float32), -bound, bound) * scale
    return values.astype(jnp.bfloat16)


def draw_inputs(key, part):
    key = jax.random.fold_in(key, 31)
    return drawn_field(key, (MB, SLOTS, LENGTH, D), 1.0, 6.0)


def draw_first_qkv(key, part):
    key = jax.random.fold_in(key, 41)
    return drawn_field(key, (D, 3 * D), D ** (-0.5), 4.0)


def draw_second_qkv(key, part):
    key = jax.random.fold_in(key, 43)
    return drawn_field(key, (D, 3 * D), D ** (-0.5), 4.0)


def draw_first_out(key, part):
    key = jax.random.fold_in(key, 47)
    return drawn_field(key, (D, D), 1.0, 4.0)


def draw_second_out(key, part):
    key = jax.random.fold_in(key, 53)
    return drawn_field(key, (D, D), 1.0, 4.0)


def level_of(rng, dims, pieces, low, high):
    level = 1.0
    for dim, blocks in pieces:
        heights = jax.random.uniform(jax.random.fold_in(jax.random.fold_in(rng, 6), dim), (blocks,), jnp.float32, low / len(pieces), high / len(pieces))
        level = level * jnp.repeat(jnp.exp(heights), dims[dim] // blocks).reshape((-1,) + (1,) * (len(dims) - 1 - dim))
    return level


def gaussian(own_key, dims, scale, most, shards=(), held_as=jnp.bfloat16):
    values = scale * jax.random.normal(own_key, dims, jnp.float32)
    if shards:
        values = values * level_of(own_key, dims, shards, -0.22, 0.18)
    return jnp.clip(values, -most, most).astype(held_as)


def setup_inputs(seed: int = 0) -> dict:
    seeds = jax.random.split(jax.random.key(seed), 22)
    return {
        "inputs": draw_inputs(jax.random.fold_in(seeds[21], 71), 0),
        "cotangent": gaussian(seeds[1], (MB, SLOTS, LENGTH, D), 1.0, 6.0, ((1, 4), (2, 8))),
        "live": draw_live(jax.random.fold_in(seeds[21], 71), 0),
        "first_qkv": draw_first_qkv(jax.random.fold_in(seeds[21], 71), 0),
        "first_out": draw_first_out(jax.random.fold_in(seeds[21], 71), 0),
        "first_gain_a": jnp.clip(1.0 + 0.18 * jax.random.normal(seeds[5], (D,), jnp.float32), 0.099609375, 1.8984375).astype(jnp.bfloat16),
        "first_shift_a": gaussian(seeds[6], (D,), 0.5, 3.0, ((0, 4),)),
        "first_gate": gaussian(seeds[7], (D, FF), D ** -0.5, 0.21875, ((0, 4),)),
        "first_up": gaussian(seeds[8], (D, FF), D ** -0.5, 0.21875, ((0, 4),)),
        "first_down": gaussian(seeds[9], (FF, D), FF ** -0.5, 0.109375, ((0, 4),)),
        "first_gain_f": jnp.clip(1.0 + 0.18 * jax.random.normal(seeds[10], (D,), jnp.float32), 0.099609375, 1.8984375).astype(jnp.bfloat16),
        "first_shift_f": gaussian(seeds[11], (D,), 0.5, 3.0, ((0, 4),)),
        "second_qkv": draw_second_qkv(jax.random.fold_in(seeds[21], 71), 0),
        "second_out": draw_second_out(jax.random.fold_in(seeds[21], 71), 0),
        "second_gain_a": jnp.clip(1.0 + 0.18 * jax.random.normal(seeds[14], (D,), jnp.float32), 0.099609375, 1.8984375).astype(jnp.bfloat16),
        "second_shift_a": gaussian(seeds[15], (D,), 0.5, 3.0, ((0, 4),)),
        "second_gate": gaussian(seeds[16], (D, FF), D ** -0.5, 0.21875, ((0, 4),)),
        "second_up": gaussian(seeds[17], (D, FF), D ** -0.5, 0.21875, ((0, 4),)),
        "second_down": gaussian(seeds[18], (FF, D), FF ** -0.5, 0.109375, ((0, 4),)),
        "second_gain_f": jnp.clip(1.0 + 0.18 * jax.random.normal(seeds[19], (D,), jnp.float32), 0.099609375, 1.8984375).astype(jnp.bfloat16),
        "second_shift_f": gaussian(seeds[20], (D,), 0.5, 3.0, ((0, 4),)),
    }


@jax.custom_vjp
def low(v):
    return lax.optimization_barrier(v.astype(jnp.bfloat16)).astype(jnp.float32)

@jax.custom_vjp
def low_back(v):
    return v

def low_keep(v):
    return (low(v), None)

def low_pass(kept, grad):
    return (grad,)

def back_keep(v):
    return (v, None)

def back_low(kept, grad):
    return (low(grad),)
low.defvjp(low_keep, low_pass)
low_back.defvjp(back_keep, back_low)

def tables(positions):
    half = HEAD // 2
    freqs = 1000.0 ** (-(jnp.arange(half).astype(jnp.float32) * 2.0 / HEAD))
    angles = positions[:, None] * freqs[None, :]
    return (jnp.cos(angles), jnp.sin(angles))

def rotate(values, cosine, sine):
    half = HEAD // 2
    first = values[..., :half]
    second = values[..., half:]
    cos_b = cosine[:, None, :]
    sin_b = sine[:, None, :]
    return jnp.concatenate([first * cos_b - second * sin_b, second * cos_b + first * sin_b], axis=-1)

def layer_norm(rows, gain, shift):
    center = rows - lax.optimization_barrier(jnp.mean(rows, axis=-1, keepdims=True))
    spread = lax.optimization_barrier(jnp.mean(center * center, axis=-1, keepdims=True))
    return center * lax.rsqrt(spread + 1e-05) * gain + shift

def attend_block(query_block, keys, values):
    scores = low_back(jnp.einsum('qhd,khd->hqk', query_block, keys, precision=lax.Precision.HIGHEST) * HEAD ** (-0.5))
    probs = jax.nn.softmax(scores, axis=-1)
    return jnp.einsum('hqk,khd->qhd', low(probs), values, precision=lax.Precision.HIGHEST)

def encoder_layer(hidden_in, weights, cosine, sine):
    w_qkv, w_out, gain_a, shift_a, w_gate, w_up, w_down, gain_f, shift_f = weights
    length = hidden_in.shape[0]
    width = hidden_in.shape[1]
    heads = width // HEAD
    act = low(hidden_in)
    joint = low_back(jnp.dot(act, w_qkv, precision=lax.Precision.HIGHEST))
    query = joint[:, :width].reshape(length, heads, HEAD)
    keys = joint[:, width:2 * width].reshape(length, heads, HEAD)
    values = joint[:, 2 * width:].reshape(length, heads, HEAD)
    query_r = low(rotate(query, cosine, sine))
    keys_r = low(rotate(keys, cosine, sine))
    values_r = low(values)
    block = min(512, length)
    blocks = query_r.reshape(length // block, block, heads, HEAD)
    context = lax.map(jax.checkpoint(lambda piece: attend_block(piece, keys_r, values_r)), blocks)
    context = low(low_back(context.reshape(length, width)))
    attn = low_back(jnp.dot(context, w_out, precision=lax.Precision.HIGHEST))
    norm_a = layer_norm(hidden_in + attn, gain_a, shift_a)
    act_f = low(norm_a)
    gate_pre = low_back(jnp.dot(act_f, w_gate, precision=lax.Precision.HIGHEST))
    up_pre = low_back(jnp.dot(act_f, w_up, precision=lax.Precision.HIGHEST))
    hidden = low(jax.nn.silu(gate_pre) * up_pre)
    branch = low_back(jnp.dot(hidden, w_down, precision=lax.Precision.HIGHEST))
    return layer_norm(norm_a + branch, gain_f, shift_f)

def run_sequence(sequence, weights):
    cosine, sine = tables(jnp.arange(sequence.shape[0]).astype(jnp.float32))
    middle = encoder_layer(sequence, weights[:9], cosine, sine)
    return encoder_layer(middle, weights[9:], cosine, sine)

def reference(inputs, cotangent, live, first_qkv, first_out, first_gain_a, first_shift_a, first_gate, first_up, first_down, first_gain_f, first_shift_f, second_qkv, second_out, second_gain_a, second_shift_a, second_gate, second_up, second_down, second_gain_f, second_shift_f):
    weights = tuple((w.astype(jnp.float32) for w in (first_qkv, first_out, first_gain_a, first_shift_a, first_gate, first_up, first_down, first_gain_f, first_shift_f, second_qkv, second_out, second_gain_a, second_shift_a, second_gate, second_up, second_down, second_gain_f, second_shift_f)))
    mask = live.astype(jnp.float32)[:, :, None, None]

    def forward(stacked, params):
        flat = stacked.reshape(MB * SLOTS, LENGTH, D)
        result = lax.map(jax.checkpoint(lambda seq_rows: run_sequence(seq_rows, params)), flat)
        return result.reshape(stacked.shape) * mask
    result, pullback = jax.vjp(forward, inputs.astype(jnp.float32), weights)
    grad_in, grads = pullback(cotangent.astype(jnp.float32))
    return (result.astype(jnp.bfloat16), grad_in.astype(jnp.bfloat16), grads[0], grads[1], grads[2], grads[3], grads[4], grads[5], grads[6], grads[7], grads[8], grads[9], grads[10], grads[11], grads[12], grads[13], grads[14], grads[15], grads[16], grads[17])
```

```python
import functools

import jax
import jax.numpy as jnp
from jax import lax
from jax.experimental import pallas as pl
from jax.experimental.pallas import tpu as pltpu
from jax.sharding import PartitionSpec as P

HEAD = 64

DP = 4
SQ = 8
TOK = 128
PART = TOK // DP
ROWS = TOK + PART
ALL = DP * ROWS
HALF = 2 * ROWS
D = 768
LEN = SQ * TOK
QB = 256
F32 = jnp.float32
BF16 = jnp.bfloat16
MESH = pl.DeviceIdType.MESH


def mm(a, b):
    return lax.dot_general(a, b, (((1,), (0,)), ((), ())), preferred_element_type=F32)


def mm_t(a, b):
    return lax.dot_general(a, b, (((1,), (1,)), ((), ())), preferred_element_type=F32)


def t_mm(a, b):
    return lax.dot_general(a, b, (((0,), (0,)), ((), ())), preferred_element_type=F32)


def low_lanes(shape):
    return lax.rem(lax.broadcasted_iota(jnp.int32, shape, len(shape) - 1), 128) < 64


def swap_halves(x):
    lane = lax.broadcasted_iota(jnp.int32, x.shape, 1)
    return jnp.where(lax.rem(lane, 64) < 32, pltpu.roll(x, 96, 1), pltpu.roll(x, 32, 1))


class Links:
    def __init__(self, send, recv):
        self.send, self.recv, self.used, self.sent = send, recv, 0, []
        self.d = lax.axis_index("dp")
        self.s = lax.axis_index("seq")
        self.x = self.d // 2
        self.core = lax.rem(self.d, 2)
        self.sib = 2 * self.x + (1 - self.core)
        self.xp = lax.rem(self.d + 2, DP)
        self.diag = lax.rem(self.sib + 2, DP)
        self.z = self.s // 2
        self.y = lax.rem(self.s, 2)
        self.dp_peers = [self.xp, self.diag, self.sib]
        self.seq_peers = [lax.rem(self.s + k, SQ) for k in range(1, SQ)]

    def enter(self, peers):
        bar = pltpu.get_barrier_semaphore()
        for p in peers:
            pl.semaphore_signal(bar, inc=1, device_id=p, device_id_type=MESH)
        pl.semaphore_wait(bar, len(peers))

    def all_peers(self):
        return [(p, self.s) for p in self.dp_peers] + [(self.d, p) for p in self.seq_peers]

    def copy(self, src, dst, to):
        i = self.used
        self.used += 1
        c = pltpu.make_async_remote_copy(
            src_ref=src,
            dst_ref=dst,
            send_sem=self.send.at[i],
            recv_sem=self.recv.at[i],
            device_id=to,
            device_id_type=MESH,
        )
        c.start()
        self.sent.append(c)
        return c

    def drain(self):
        for c in self.sent:
            c.wait_send()


def block(ref, i, rows=ROWS):
    return ref.at[pl.ds(pl.multiple_of(i * rows, 16), rows)]


def gather_begin(L, ref, rows=ROWS):
    own = block(ref, L.d, rows)
    far = L.copy(own, own, (L.xp, L.s))
    near = L.copy(own, own, (L.sib, L.s))
    return near, far


def gather_forward(L, ref, far, rows=ROWS):
    far.wait_recv()
    got = block(ref, L.xp, rows)
    return L.copy(got, got, (L.sib, L.s))


def reduce_own(L, part, bufs):
    snd, got, mid, fin = bufs
    snd[0] = block(part, L.sib)[...].astype(BF16)
    return L.copy(snd.at[0], got.at[0], (L.sib, L.s))


def reduce_other(L, part, bufs):
    snd, got, mid, fin = bufs
    snd[1] = block(part, L.diag)[...].astype(BF16)
    return L.copy(snd.at[1], got.at[1], (L.sib, L.s))


def reduce_cross(L, part, bufs, c_other):
    snd, got, mid, fin = bufs
    c_other.wait_recv()
    mid[...] = (block(part, L.xp)[...] + got[1].astype(F32)).astype(BF16)
    return L.copy(mid, fin, (L.xp, L.s))


def reduce_end(L, part, bufs, c_own, c_cross):
    snd, got, mid, fin = bufs
    c_own.wait_recv()
    c_cross.wait_recv()
    return block(part, L.d)[...] + got[0].astype(F32) + fin[...].astype(F32)


REDUCE_BUFS = [
    pltpu.VMEM((2, ROWS, D), BF16),
    pltpu.VMEM((2, ROWS, D), BF16),
    pltpu.VMEM((ROWS, D), BF16),
    pltpu.VMEM((ROWS, D), BF16),
]


def chip_rows(c):
    return pl.ds(pl.multiple_of(c * HALF, 32), HALF)


def token_rows(s):
    return pl.ds(pl.multiple_of(s * TOK, TOK), TOK)


def normalize(res):
    cen = res - jnp.mean(res, axis=-1, keepdims=True)
    rstd = lax.rsqrt(jnp.mean(cen * cen, axis=-1, keepdims=True) + 1e-05)
    return cen * rstd, rstd


def normalize_back(grad, gain, xhat, rstd):
    dn = grad * gain
    return (dn - jnp.mean(dn, axis=-1, keepdims=True) - xhat * jnp.mean(dn * xhat, axis=-1, keepdims=True)) * rstd


def pack_pairs(src, dst):
    half = dst.shape[-1]
    one, two = pl.ds(0, half), pl.ds(half, half)
    keep = low_lanes((TOK, half))
    for e in range(DP):
        dst[e] = src[pl.ds(ROWS * e, TOK), one]
        dst[4, pl.ds(PART * e, PART)] = src[pl.ds(ROWS * e + TOK, PART), one]
        dst[7, pl.ds(PART * e, PART)] = src[pl.ds(ROWS * e + TOK, PART), two]
    for p in range(2):
        a = src[pl.ds(ROWS * 2 * p, TOK), two].astype(F32)
        b = src[pl.ds(ROWS * (2 * p + 1), TOK), two].astype(F32)
        dst[5 + p] = jnp.where(keep, a, b).astype(BF16)


def unpack_pairs(src, dst):
    half = src.shape[-1]
    one, two = pl.ds(0, half), pl.ds(half, half)
    keep = low_lanes((TOK, half))
    third = [src[5].astype(F32), src[6].astype(F32)]
    last = jnp.where(keep, src[7].astype(F32), 0.0).astype(BF16)
    for e in range(DP):
        dst[pl.ds(ROWS * e, TOK), one] = src[e]
        mine = third[e // 2]
        mine = jnp.where(keep, mine, 0.0) if e % 2 == 0 else jnp.where(keep, 0.0, mine)
        dst[pl.ds(ROWS * e, TOK), two] = mine.astype(BF16)
        dst[pl.ds(ROWS * e + TOK, PART), one] = src[4, pl.ds(PART * e, PART)]
        dst[pl.ds(ROWS * e + TOK, PART), two] = last[PART * e : PART * (e + 1)]


def forward_kernel(first, layer, *refs):
    if first:
        (inp, livet, cot, nvp, wqs, wg, wu, wo, wd, cosr, sinr) = refs[:11]
        (o_h, o_x, o_qkv, o_lse, o_ctx, o_ce, o_actf, o_gp, o_up, o_hid, o_xa, o_xf, o_ra, o_rf, o_wq, o_wg, o_wu, o_wo, o_cot, o_lv, o_nv) = refs[11:32]
        rest = refs[32:]
        (inb, cbuf, nbuf) = rest[:3]
        rest = rest[3:]
        nv = o_nv
    else:
        (hin, nv, wqs, wg, wu, wo, wd, cosr, sinr) = refs[:9]
        (o_h, o_x, o_qkv, o_lse, o_ctx, o_ce, o_actf, o_gp, o_up, o_hid, o_xa, o_xf, o_ra, o_rf, o_wq, o_wg, o_wu, o_wo) = refs[9:27]
        rest = refs[27:]
    (part, qx, sbq, cbk, crx, kz) = rest[:6]
    red_a, red_f = rest[6:10], rest[10:14]
    send, recv, lsem = rest[14:17]
    L = Links(send, recv)
    L.enter(L.all_peers())
    d, s = L.d, L.s
    depth = D // DP

    if first:
        inb[pl.ds(pl.multiple_of(d * 256, 256), 256)] = inp[...].reshape(256, D)
        o_lv[d] = livet[...]
        nbuf[d] = nvp[...]
        small = []
        for p in L.dp_peers:
            small.append(L.copy(livet, o_lv.at[d], (p, s)))
            small.append(L.copy(nvp, nbuf.at[d], (p, s)))
        near, far = gather_begin(L, inb, 256)
    else:
        block(o_x, d)[...] = hin[...].astype(BF16)
        near, far = gather_begin(L, o_x)

    own = pl.ds(pl.multiple_of(d * depth, 64), depth)
    qw = [L.copy(wqs.at[p], o_wq.at[own], (p, s)) for p in L.dp_peers]
    o_wq[own] = wqs[d]
    cols = [pl.ds(pl.multiple_of(p * D, D), D) for p in L.dp_peers]
    mine = pl.ds(pl.multiple_of(d * D, D), D)
    loc = [
        pltpu.make_async_copy(wg.at[:, mine], o_wg.at[own], lsem.at[0]),
        pltpu.make_async_copy(wu.at[:, mine], o_wu.at[own], lsem.at[1]),
    ]
    for c in loc:
        c.start()
    o_wo[pl.ds(0, depth)] = wo[...]
    o_wo[pl.ds(depth, 64)] = wo[pl.ds(128, 64)]

    def project(rows):
        y = mm(o_x[rows], o_wq[...])
        co, si = cosr[rows], sinr[rows]
        for t in range(6):
            v = y[:, 128 * t : 128 * (t + 1)]
            if t % 3 != 2:
                v = v * co + swap_halves(v) * si
            if t % 3 == 0:
                v = v * (HEAD**-0.5)
            qx[rows, pl.ds(128 * t, 128)] = v.astype(BF16)

    fwd = gather_forward(L, inb if first else o_x, far, 256 if first else ROWS)
    near.wait_recv()
    if first:
        for c in small:
            c.wait_recv()
        o_nv[...] = nbuf[0] + nbuf[1] + nbuf[2] + nbuf[3]
        f0 = o_lv[0, 0:1] * o_lv[1, 0:1] * o_lv[2, 0:1] * o_lv[3, 0:1]
        f1 = 1.0 - f0
        fwd.wait_recv()
        own_lone = [f0 * o_lv[j, 1:2] + f1 * o_lv[j, 0:1] for j in range(DP)]
        lone = None
        for j in range(DP):
            a = inb[pl.ds(256 * j, TOK)].astype(F32)
            b = inb[pl.ds(256 * j + TOK, TOK)].astype(F32)
            o_x[pl.ds(ROWS * j, TOK)] = (f0 * a + f1 * b).astype(BF16)
            term = own_lone[j] * (f0 * b + f1 * a)
            lone = term if lone is None else lone + term
        lone = lone.astype(BF16)
        for j in range(DP):
            o_x[pl.ds(ROWS * j + TOK, PART)] = lone[PART * j : PART * (j + 1)]
        for c in qw:
            c.wait_recv()
        project(chip_rows(0))
        project(chip_rows(1))
    else:
        for c in qw:
            c.wait_recv()
        project(chip_rows(L.x))
        fwd.wait_recv()
        project(chip_rows(1 - L.x))

    pack_pairs(qx, sbq)
    o_qkv[token_rows(s)] = sbq[s]
    qc = [L.copy(sbq.at[p], o_qkv.at[token_rows(s)], (d, p)) for p in L.seq_peers]
    gw = [L.copy(wg.at[:, c], o_wg.at[own], (p, s)) for p, c in zip(L.dp_peers, cols)]
    gw += [L.copy(wu.at[:, c], o_wu.at[own], (p, s)) for p, c in zip(L.dp_peers, cols)]
    if first:
        cbuf[d] = cot[:, token_part(d), :]
        cc = [L.copy(cot.at[:, token_part(p), :], cbuf.at[d], (p, s)) for p in L.dp_peers]
    for c in qc:
        c.wait_recv()

    keep = low_lanes((LEN, 128))
    k = o_qkv[:, pl.ds(128, 128)].astype(F32)
    kz[0] = jnp.where(keep, k, 0.0).astype(BF16)
    kz[1] = jnp.where(keep, 0.0, k).astype(BF16)

    @pl.loop(0, LEN // QB)
    def _(i):
        at = pl.ds(pl.multiple_of(i * QB, QB), QB)
        q = o_qkv[at, pl.ds(0, 128)]
        outs, logs = [], []
        for j in range(2):
            sc = mm_t(q, kz[j])
            top = jnp.max(sc, axis=-1, keepdims=True)
            ex = jnp.exp(sc - top)
            tot = jnp.sum(ex, axis=-1, keepdims=True)
            o = mm(ex.astype(BF16), o_qkv[:, pl.ds(256, 128)])
            outs.append(o / tot)
            logs.append(jnp.broadcast_to(top + jnp.log(tot), (QB, 128)))
        pick = low_lanes((QB, 128))
        ctx = jnp.where(pick, outs[0], outs[1])
        o_ctx[at] = ctx
        o_lse[at] = jnp.where(pick, logs[0], logs[1])
        cbk[at] = ctx.astype(BF16)

    crx[s] = cbk[token_rows(s)]
    bc = [L.copy(cbk.at[token_rows(p)], crx.at[s], (d, p)) for p in L.seq_peers]
    if first:
        for c in cc:
            c.wait_recv()
        a = cot[0].astype(F32)
        b = cot[1].astype(F32)
        o_cot[pl.ds(0, TOK)] = f0 * a + f1 * b
        lone = None
        for j in range(DP):
            term = own_lone[j] * (f0 * cbuf[j, 1].astype(F32) + f1 * cbuf[j, 0].astype(F32))
            lone = term if lone is None else lone + term
        o_cot[pl.ds(TOK, PART)] = lone
    for c in bc:
        c.wait_recv()
    unpack_pairs(crx, o_ce)

    for c in (1 - L.x, L.x):
        rows = chip_rows(c)
        part[rows] = mm(o_ce[rows], o_wo[...])
    c_other = reduce_other(L, part, red_a)
    c_own = reduce_own(L, part, red_a)
    c_cross = reduce_cross(L, part, red_a, c_other)
    attn = reduce_end(L, part, red_a, c_own, c_cross)
    if first:
        res = block(o_x, d)[...].astype(F32) + attn
    else:
        res = hin[...] + attn
    base = 4 * layer
    xhat, rstd = normalize(res)
    norm_a = xhat * nv[base : base + 1] + nv[base + 1 : base + 2]
    block(o_actf, d)[...] = norm_a.astype(BF16)
    near, far = gather_begin(L, o_actf)
    o_xa[...] = xhat
    o_ra[...] = jnp.broadcast_to(rstd, (ROWS, 128))
    for c in loc:
        c.wait()
    for c in gw:
        c.wait_recv()

    def feed(rows):
        a = o_actf[rows]
        gp = mm(a, o_wg[...])
        up = mm(a, o_wu[...])
        o_gp[rows] = gp
        o_up[rows] = up
        hid = (gp * jax.nn.sigmoid(gp) * up).astype(BF16)
        o_hid[rows] = hid
        part[rows] = mm(hid, wd[...])

    near.wait_recv()
    feed(chip_rows(L.x))
    c_own = reduce_own(L, part, red_f)
    fwd = gather_forward(L, o_actf, far)
    fwd.wait_recv()
    feed(chip_rows(1 - L.x))
    c_other = reduce_other(L, part, red_f)
    c_cross = reduce_cross(L, part, red_f, c_other)
    res = norm_a + reduce_end(L, part, red_f, c_own, c_cross)
    xhat, rstd = normalize(res)
    o_h[...] = xhat * nv[base + 2 : base + 3] + nv[base + 3 : base + 4]
    o_xf[...] = xhat
    o_rf[...] = jnp.broadcast_to(rstd, (ROWS, 128))
    L.drain()


def token_part(p):
    return pl.ds(pl.multiple_of(p * PART, PART), PART)


def backward_kernel(layer, *refs):
    (gin, nv, x, qkv, lse, ctx, ce, actf, gp, up, hid, xa, xf, ra, rf, wq, wg, wu, wo, wd, cosf, sinf, v_in) = refs[:23]
    (o_g, o_w, o_v) = refs[23:26]
    (part, db, dg, du, dsb, dc, sbq, dback, drx, dqkv, kz, vz, kt, lt, et, dkv, dqt) = refs[26:43]
    red_f, red_a = refs[43:47], refs[47:51]
    send, recv = refs[51:53]
    L = Links(send, recv)
    L.enter([(p, L.s) for p in (L.xp, L.sib)] + [(L.d, p) for p in L.seq_peers])
    d, s = L.d, L.s
    base = 4 * layer

    o_v[...] = v_in[...]
    grad = gin[...]
    xhat = xf[...]
    d_res_f = normalize_back(grad, nv[base + 2 : base + 3], xhat, rf[:, 0:1])
    block(db, d)[...] = d_res_f.astype(BF16)
    near, far = gather_begin(L, db)
    o_v[base + 2 : base + 3] = jnp.sum(grad * xhat, axis=0, keepdims=True)
    o_v[base + 3 : base + 4] = jnp.sum(grad, axis=0, keepdims=True)

    def feed(rows):
        dh = mm_t(db[rows], wd[...])
        g, u = gp[rows], up[rows]
        sig = jax.nn.sigmoid(g)
        dgv = (dh * u * sig * (1.0 + g * (1.0 - sig))).astype(BF16)
        duv = (dh * g * sig).astype(BF16)
        dg[rows] = dgv
        du[rows] = duv
        part[rows] = mm_t(dgv, wg[...]) + mm_t(duv, wu[...])

    near.wait_recv()
    feed(chip_rows(L.x))
    c_own = reduce_own(L, part, red_f)
    fwd = gather_forward(L, db, far)
    fwd.wait_recv()
    feed(chip_rows(1 - L.x))
    c_other = reduce_other(L, part, red_f)
    c_cross = reduce_cross(L, part, red_f, c_other)
    quarter = D // DP
    o_w[pl.ds(12, 4)] = t_mm(hid[...], db[...]).astype(BF16).reshape(4, quarter, D)
    o_w[pl.ds(4, 4)] = t_mm(actf[...], dg[...]).astype(BF16).reshape(4, quarter, D)
    o_w[pl.ds(8, 4)] = t_mm(actf[...], du[...]).astype(BF16).reshape(4, quarter, D)
    d_norm = d_res_f + reduce_end(L, part, red_f, c_own, c_cross)
    xhat = xa[...]
    d_res_a = normalize_back(d_norm, nv[base : base + 1], xhat, ra[:, 0:1])

    block(dsb, d)[...] = d_res_a.astype(BF16)
    near, far = gather_begin(L, dsb)
    o_v[base : base + 1] = jnp.sum(d_norm * xhat, axis=0, keepdims=True)
    o_v[base + 1 : base + 2] = jnp.sum(d_norm, axis=0, keepdims=True)
    fwd = gather_forward(L, dsb, far)
    near.wait_recv()
    fwd.wait_recv()
    dg[:, pl.ds(0, 256)] = mm_t(dsb[...], wo[...]).astype(BF16)
    pack_pairs(dg.at[:, pl.ds(0, 256)], sbq)
    dc[token_rows(s)] = sbq[s]
    qc = [L.copy(sbq.at[p], dc.at[token_rows(s)], (d, p)) for p in L.seq_peers]

    g_out = t_mm(ce[...], dsb[...])
    o_w[16, pl.ds(0, 128)] = g_out[0:128].astype(BF16)
    o_w[16, pl.ds(128, 64)] = (g_out[128:192] + g_out[192:256]).astype(BF16)

    keep = low_lanes((LEN, 128))
    k = qkv[:, pl.ds(128, 128)].astype(F32)
    kz[0] = jnp.where(keep, k, 0.0).astype(BF16)
    kz[1] = jnp.where(keep, 0.0, k).astype(BF16)
    kt[0] = kz[0].astype(F32).T.astype(BF16)
    kt[1] = kz[1].astype(F32).T.astype(BF16)
    v = qkv[:, pl.ds(256, 128)].astype(F32)
    vz[0] = jnp.where(keep, v, 0.0).astype(BF16)
    vz[1] = jnp.where(keep, 0.0, v).astype(BF16)
    lt[...] = lse[...].T
    for c in qc:
        c.wait_recv()
    et[...] = (dc[...].astype(F32) * ctx[...]).T
    dkv[...] = jnp.zeros_like(dkv)
    pick = low_lanes((QB, 128))

    @pl.loop(0, LEN // QB)
    def _(i):
        at = pl.ds(pl.multiple_of(i * QB, QB), QB)
        q = qkv[at, pl.ds(0, 128)]
        g = dc[at]
        qf, gf = q.astype(F32), g.astype(F32)
        acc = None
        for j in range(2):
            qz = (jnp.where(pick, qf, 0.0) if j == 0 else jnp.where(pick, 0.0, qf)).astype(BF16)
            gz = (jnp.where(pick, gf, 0.0) if j == 0 else jnp.where(pick, 0.0, gf)).astype(BF16)
            log = lt[pl.ds(64 * j, 1), at]
            inner = jnp.sum(et[pl.ds(64 * j, 64), at], axis=0, keepdims=True)
            pr = jnp.exp(mm_t(kz[j], q) - log)
            dp = mm_t(vz[j], g)
            ds = (pr * (dp - inner)).astype(BF16)
            dkv[:, pl.ds(128, 128)] += mm(pr.astype(BF16), gz)
            dkv[:, pl.ds(0, 128)] += mm(ds, qz)
            term = mm(kt[j], ds)
            acc = term if acc is None else acc + term
        dqt[:, at] = acc

    def unrotate(g):
        return g * cosf[...] - swap_halves(g) * sinf[...]

    dback[:, pl.ds(0, 128)] = unrotate(dqt[...].T * (HEAD**-0.5)).astype(BF16)
    dback[:, pl.ds(128, 128)] = unrotate(dkv[:, pl.ds(0, 128)]).astype(BF16)
    dback[:, pl.ds(256, 128)] = dkv[:, pl.ds(128, 128)].astype(BF16)
    drx[s] = dback[token_rows(s)]
    bc = [L.copy(dback.at[token_rows(p)], drx.at[s], (d, p)) for p in L.seq_peers]
    for c in bc:
        c.wait_recv()
    unpack_pairs(drx, dqkv)
    for c in (1 - L.x, L.x):
        rows = chip_rows(c)
        part[rows] = mm_t(dqkv[rows], wq[...])
    c_other = reduce_other(L, part, red_a)
    c_own = reduce_own(L, part, red_a)
    c_cross = reduce_cross(L, part, red_a, c_other)
    o_w[pl.ds(0, 4)] = t_mm(x[...], dqkv[...]).astype(BF16).reshape(4, quarter, D)
    o_g[...] = d_res_a + reduce_end(L, part, red_a, c_own, c_cross)
    L.drain()


BLOCKS = 17
CHUNKS = [(0, 4), (4, 4), (8, 4), (12, 5)]
ZS = 4
ZR = D // DP // ZS
YC = D // 2


def reduce_kernel(*refs):
    (w1, w2, vin, lone) = refs[:4]
    (f1, f2, o_v, o_lone) = refs[4:8]
    bufs = [refs[8:12], refs[12:16]]
    (vy, vz, vs, vx, va, vb, vc) = refs[16:23]
    send, recv = refs[23:25]
    L = Links(send, recv)
    d, s, y, z = L.d, L.s, L.y, L.z
    yp = 2 * z + (1 - y)
    zps = [lax.rem(z + k, ZS) for k in range(1, ZS)]
    zdev = [(d, 2 * p + y) for p in zps]
    L.enter([(p, s) for p in L.dp_peers] + [(d, yp)] + zdev)
    mine = pl.ds(pl.multiple_of(y * YC, 128), YC)
    theirs = pl.ds(pl.multiple_of((1 - y) * YC, 128), YC)
    zrows = pl.ds(pl.multiple_of(z * ZR, ZR), ZR)

    o_lone[d] = lone[...]
    lc = [L.copy(lone, o_lone.at[d], (p, s)) for p in L.dp_peers]
    vcp = L.copy(vin, vy, (d, yp))
    jobs = []
    for w, f, (ry, h, rz, sm) in ((w2, f2, bufs[1]), (w1, f1, bufs[0])):
        for at, n in CHUNKS:
            jobs.append((w, f, ry, h, rz, sm, at, n))
    ys = [L.copy(w.at[pl.ds(at, n), :, theirs], ry.at[pl.ds(at, n)], (d, yp)) for (w, f, ry, h, rz, sm, at, n) in jobs]
    vcp.wait_recv()
    va[...] = vin[...] + vy[...]
    vzc = [L.copy(va, vz.at[k], zdev[k]) for k in range(ZS - 1)]
    zs = []
    for c, (w, f, ry, h, rz, sm, at, n) in zip(ys, jobs):
        r = pl.ds(at, n)
        c.wait_recv()
        h[r] = (w[r, :, mine].astype(F32) + ry[r].astype(F32)).astype(BF16)
        zs.append(
            [
                L.copy(h.at[r, pl.ds(pl.multiple_of(zps[k] * ZR, ZR), ZR)], rz.at[k, r], zdev[k])
                for k in range(ZS - 1)
            ]
        )
    for c in vzc:
        c.wait_recv()
    vb[...] = va[...] + vz[0] + vz[1] + vz[2]
    vsc = L.copy(vb, vs, (L.sib, s))
    ds = []
    for cs, (w, f, ry, h, rz, sm, at, n) in zip(zs, jobs):
        r = pl.ds(at, n)
        for c in cs:
            c.wait_recv()
        total = h[r, zrows].astype(F32)
        for k in range(ZS - 1):
            total = total + rz[k, r].astype(F32)
        if n == 4:
            sm[r] = total.astype(BF16)
            f[y, at + d, zrows] = sm[at + d]
            ds.append([L.copy(sm.at[at + p], f.at[y, at + d, zrows], (p, s)) for p in L.dp_peers])
        else:
            f[y, r, zrows] = total.astype(BF16)
            ds.append([])
    vsc.wait_recv()
    vc[...] = vb[...] + vs[...]
    vxc = L.copy(vc, vx, (L.xp, s))
    gs = []
    for cs, (w, f, ry, h, rz, sm, at, n) in zip(ds, jobs):
        r = pl.ds(at, n)
        for c in cs:
            c.wait_recv()
        gs.append([L.copy(f.at[y, r, zrows], f.at[y, r, zrows], p) for p in zdev])
    es = []
    for cs, (w, f, ry, h, rz, sm, at, n) in zip(gs, jobs):
        r = pl.ds(at, n)
        for c in cs:
            c.wait_recv()
        es.append(L.copy(f.at[y, r], f.at[y, r], (d, yp)))
    for c in es + lc:
        c.wait_recv()
    vxc.wait_recv()
    o_v[...] = vc[...] + vx[...]
    L.drain()


def sds(shape, dtype):
    return jax.ShapeDtypeStruct(shape, dtype)


def call(body, name, cid, outs, scratch, flops, args, anyargs=()):
    return pl.pallas_call(
        body,
        name=name,
        out_shape=[sds(*o) for o in outs],
        in_specs=[
            pl.BlockSpec(memory_space=pl.ANY if i in anyargs else pltpu.VMEM) for i in range(len(args))
        ],
        out_specs=[pl.BlockSpec(memory_space=pltpu.VMEM)] * len(outs),
        scratch_shapes=scratch,
        cost_estimate=pl.CostEstimate(flops=flops, bytes_accessed=2 * 10**7, transcendentals=10**6),
        compiler_params=pltpu.CompilerParams(
            collective_id=cid, has_side_effects=True, vmem_limit_bytes=58 * 2**20
        ),
    )(*args)


SAVED = [
    ((ALL, D), BF16),
    ((LEN, 384), BF16),
    ((LEN, 128), F32),
    ((LEN, 128), F32),
    ((ALL, 256), BF16),
    ((ALL, D), BF16),
    ((ALL, D), F32),
    ((ALL, D), F32),
    ((ALL, D), BF16),
    ((ROWS, D), F32),
    ((ROWS, D), F32),
    ((ROWS, 128), F32),
    ((ROWS, 128), F32),
    ((D, D), BF16),
    ((D, D), BF16),
    ((D, D), BF16),
    ((256, D), BF16),
]


def run_forward(first, layer, args, anyargs):
    outs = [((ROWS, D), F32)] + SAVED
    scratch = []
    if first:
        outs = outs + [((ROWS, D), F32), ((DP, 8, D), F32), ((8, D), F32)]
        scratch = [
            pltpu.VMEM((DP * 256, D), BF16),
            pltpu.VMEM((DP, 2, PART, D), BF16),
            pltpu.VMEM((DP, 8, D), F32),
        ]
    scratch = scratch + [
        pltpu.VMEM((ALL, D), F32),
        pltpu.VMEM((ALL, D), BF16),
        pltpu.VMEM((SQ, TOK, 384), BF16),
        pltpu.VMEM((LEN, 128), BF16),
        pltpu.VMEM((SQ, TOK, 128), BF16),
        pltpu.VMEM((2, LEN, 128), BF16),
    ]
    scratch = scratch + REDUCE_BUFS + REDUCE_BUFS
    scratch += [pltpu.SemaphoreType.DMA((64,)), pltpu.SemaphoreType.DMA((64,)), pltpu.SemaphoreType.DMA((2,))]
    body = functools.partial(forward_kernel, first, layer)
    return call(body, "fwd" + str(layer), 1 + layer, outs, scratch, 6 * 10**9, args, anyargs)


def run_backward(layer, args):
    outs = [((ROWS, D), F32), ((BLOCKS, D // DP, D), BF16), ((8, D), F32)]
    scratch = [
        pltpu.VMEM((ALL, D), F32),
        pltpu.VMEM((ALL, D), BF16),
        pltpu.VMEM((ALL, D), BF16),
        pltpu.VMEM((ALL, D), BF16),
        pltpu.VMEM((ALL, D), BF16),
        pltpu.VMEM((LEN, 128), BF16),
        pltpu.VMEM((SQ, TOK, 128), BF16),
        pltpu.VMEM((LEN, 384), BF16),
        pltpu.VMEM((SQ, TOK, 384), BF16),
        pltpu.VMEM((ALL, D), BF16),
        pltpu.VMEM((2, LEN, 128), BF16),
        pltpu.VMEM((2, LEN, 128), BF16),
        pltpu.VMEM((2, 128, LEN), BF16),
        pltpu.VMEM((128, LEN), F32),
        pltpu.VMEM((128, LEN), F32),
        pltpu.VMEM((LEN, 256), F32),
        pltpu.VMEM((128, LEN), F32),
    ]
    scratch = scratch + REDUCE_BUFS + REDUCE_BUFS
    scratch += [pltpu.SemaphoreType.DMA((64,)), pltpu.SemaphoreType.DMA((64,))]
    body = functools.partial(backward_kernel, layer)
    return call(body, "bwd" + str(layer), 3 + layer, outs, scratch, 12 * 10**9, args)


def run_reduce(args):
    quarter = D // DP
    outs = [((2, BLOCKS, quarter, YC), BF16)] * 2 + [((8, D), F32), ((DP, 2, PART, D), BF16)]
    one = [
        pltpu.VMEM((BLOCKS, quarter, YC), BF16),
        pltpu.VMEM((BLOCKS, quarter, YC), BF16),
        pltpu.VMEM((ZS - 1, BLOCKS, ZR, YC), BF16),
        pltpu.VMEM((12, ZR, YC), BF16),
    ]
    row = pltpu.VMEM((8, D), F32)
    scratch = one + one + [row, pltpu.VMEM((ZS - 1, 8, D), F32)] + [row] * 5
    scratch += [pltpu.SemaphoreType.DMA((128,)), pltpu.SemaphoreType.DMA((128,))]
    return call(reduce_kernel, "wsum", 5, outs, scratch, 10**8, args)


def spread_qkv(w):
    depth = w.shape[0]
    w = w.reshape(depth, 3, DP, 192).transpose(2, 0, 1, 3)
    pair = w[..., :128].reshape(DP, depth, 384)
    third = w[..., 128:]
    third = jnp.concatenate([third, third], axis=-1).reshape(DP, depth, 384)
    return jnp.concatenate([pair, third], axis=-1)


def rotary():
    half = HEAD // 2
    freqs = 1000.0 ** (-(jnp.arange(half).astype(F32) * 2.0 / HEAD))
    angles = jnp.arange(LEN).astype(F32)[:, None] * freqs[None, :]
    co, si = jnp.cos(angles), jnp.sin(angles)
    return jnp.concatenate([co] * 4, axis=1), jnp.concatenate([-si, si, -si, si], axis=1)


def own_rows(table, s):
    mine = lax.dynamic_slice_in_dim(table, s * TOK, TOK, 0)
    parts = []
    for j in range(DP):
        parts += [mine, mine[PART * j : PART * (j + 1)]]
    return jnp.concatenate(parts, axis=0)


def final_grads(f):
    f = f.astype(F32)
    quarter = D // DP
    pair = f[0, 0:4].reshape(DP, quarter, 3, 128)
    third = f[1, 0:4].reshape(DP, quarter, 3, 2, 64).sum(axis=3)
    g_qkv = jnp.concatenate([pair, third], axis=-1).transpose(1, 2, 0, 3).reshape(quarter, 3 * D)
    g_gate = f[:, 4:8].transpose(2, 1, 0, 3).reshape(quarter, DP * D)
    g_up = f[:, 8:12].transpose(2, 1, 0, 3).reshape(quarter, DP * D)
    g_down = f[:, 12:16].transpose(1, 2, 0, 3).reshape(D, D)
    g_out = f[:, 16].transpose(1, 0, 2).reshape(quarter, D)
    return g_qkv, g_out, g_gate, g_up, g_down


def shared_device(inputs, cotangent, live, *weights):
    sets = (weights[:9], weights[9:])
    d, s = lax.axis_index("dp"), lax.axis_index("seq")
    cosf, sinf = rotary()
    cosr, sinr = own_rows(cosf, s), own_rows(sinf, s)
    livet = jnp.broadcast_to(jnp.pad(live[:, 0].astype(F32), (0, 6))[:, None], (8, D))
    norms = jnp.stack([sets[i][j] for i in range(2) for j in (2, 3, 7, 8)]).astype(F32)
    norms = lax.dynamic_update_slice(jnp.zeros((8, D), F32), norms, (0, d * (D // DP)))
    sends = [spread_qkv(w[0]) for w in sets]

    args = (inputs[:, 0], livet, cotangent[:, 0], norms, sends[0], sets[0][4], sets[0][5], sets[0][1], sets[0][6], cosr, sinr)
    res = run_forward(True, 0, args, (5, 6))
    h1, saved1 = res[0], res[1:18]
    gcot, lv, nv = res[18:]
    args = (h1, nv, sends[1], sets[1][4], sets[1][5], sets[1][1], sets[1][6], cosr, sinr)
    res = run_forward(False, 1, args, (3, 4))
    h2, saved2 = res[0], res[1:18]
    g, w2, v2 = run_backward(1, (gcot, nv) + tuple(saved2) + (sets[1][6], cosf, sinf, jnp.zeros((8, D), F32)))
    g, w1, v1 = run_backward(0, (g, nv) + tuple(saved1) + (sets[0][6], cosf, sinf, v2))
    out_rows = h2.astype(BF16)
    in_rows = g.astype(BF16)
    f1, f2, vsum, lone = run_reduce((w1, w2, v1, jnp.stack([out_rows[TOK:], in_rows[TOK:]])))

    full0 = lv[:, 0, 0].min() > 0.5
    here = jnp.where(full0, live[1, 0], live[0, 0]) > 0

    def place(rows, k):
        part = lone[:, k].reshape(TOK, D)
        part = jnp.where(here, part, jnp.zeros_like(part))
        whole = rows[:TOK]
        return jnp.stack([jnp.where(full0, whole, part), jnp.where(full0, part, whole)])[:, None]

    vsum = lax.dynamic_slice_in_dim(vsum, d * (D // DP), D // DP, 1)
    out = [place(out_rows, 0), place(in_rows, 1)]
    for i, f in enumerate((f1, f2)):
        g_qkv, g_out, g_gate, g_up, g_down = final_grads(f)
        v = vsum[4 * i : 4 * i + 4]
        out += [g_qkv, g_out, v[0], v[1], g_gate, g_up, g_down, v[2], v[3]]
    return tuple(out)


def fits(mesh):
    return mesh.shape["dp"] == DP and mesh.shape["seq"] == SQ


def as_sent(array):
    return jax.tree.map(lambda a: a.astype(jnp.bfloat16) if a.dtype == jnp.float32 else a, array)


def tables(positions):
    half = HEAD // 2
    freqs = 1000.0 ** (-(jnp.arange(half).astype(jnp.float32) * 2.0 / HEAD))
    angles = positions[:, None] * freqs[None, :]
    return (jnp.cos(angles), jnp.sin(angles))


def rotate(values, cosine, sine):
    half = HEAD // 2
    first = values[..., :half]
    second = values[..., half:]
    cos_b = cosine[:, None, :]
    sin_b = sine[:, None, :]
    return jnp.concatenate(
        [first * cos_b - second * sin_b, second * cos_b + first * sin_b], axis=-1
    )


def unrotate(values, cosine, sine):
    half = HEAD // 2
    first = values[..., :half]
    second = values[..., half:]
    cos_b = cosine[:, None, :]
    sin_b = sine[:, None, :]
    return jnp.concatenate(
        [first * cos_b + second * sin_b, second * cos_b - first * sin_b], axis=-1
    )


def layer_norm(rows, gain, shift):
    center = rows - jnp.mean(rows, axis=-1, keepdims=True)
    spread = jnp.mean(center * center, axis=-1, keepdims=True)
    return center * lax.rsqrt(spread + 1e-05) * gain + shift


def dot_first(left, right):
    return lax.dot_general(
        left, right, (((0,), (0,)), ((), ())), preferred_element_type=jnp.float32
    )


def dot_last(left, right):
    return lax.dot_general(
        left, right, (((1,), (1,)), ((), ())), preferred_element_type=jnp.float32
    )


def forward_layer(hidden_in, weights, cosine, sine):
    w_qkv, w_out, gain_a, shift_a, w_gate, w_up, w_down, gain_f, shift_f = weights
    tokens = hidden_in.shape[0]
    width = hidden_in.shape[1]
    heads = width // HEAD
    scale = HEAD ** (-0.5)
    act = hidden_in.astype(jnp.bfloat16)
    joint = jnp.dot(act, w_qkv, preferred_element_type=jnp.float32)
    query = joint[:, :width].reshape(tokens, heads, HEAD)
    keys = joint[:, width : 2 * width].reshape(tokens, heads, HEAD)
    query_r = rotate(query, cosine, sine).astype(jnp.bfloat16)
    keys_r = rotate(keys, cosine, sine).astype(jnp.bfloat16).reshape(tokens, width)
    values_r = joint[:, 2 * width :].astype(jnp.bfloat16)
    keys_all, values_all = (
        lax.all_gather(keys_r, "seq", axis=0, tiled=True),
        lax.all_gather(values_r, "seq", axis=0, tiled=True),
    )
    length = keys_all.shape[0]
    keys_all = keys_all.reshape(length, heads, HEAD)
    values_all = values_all.reshape(length, heads, HEAD)
    scores = (
        jnp.einsum("qhd,khd->hqk", query_r, keys_all, preferred_element_type=jnp.float32) * scale
    )
    top = jnp.max(scores, axis=-1, keepdims=True)
    expo = jnp.exp(scores - top)
    total = jnp.sum(expo, axis=-1, keepdims=True)
    probs = expo / total
    log_total = top + jnp.log(total)
    context = jnp.einsum(
        "hqk,khd->qhd", probs.astype(jnp.bfloat16), values_all, preferred_element_type=jnp.float32
    )
    context = context.reshape(tokens, width).astype(jnp.bfloat16)
    res_a = hidden_in + jnp.dot(context, w_out, preferred_element_type=jnp.float32)
    norm_a = layer_norm(res_a, gain_a.astype(jnp.float32), shift_a.astype(jnp.float32))
    act_f = norm_a.astype(jnp.bfloat16)
    gate_pre = jnp.dot(act_f, w_gate, preferred_element_type=jnp.float32)
    up_pre = jnp.dot(act_f, w_up, preferred_element_type=jnp.float32)
    hidden = (jax.nn.silu(gate_pre) * up_pre).astype(jnp.bfloat16)
    res_f = norm_a + jnp.dot(hidden, w_down, preferred_element_type=jnp.float32)
    result = layer_norm(res_f, gain_f.astype(jnp.float32), shift_f.astype(jnp.float32))
    saved = (
        act,
        query_r,
        keys_r,
        values_r,
        log_total,
        context,
        res_a,
        act_f,
        gate_pre,
        up_pre,
        hidden,
        res_f,
    )
    return (result, saved)


def backward_layer(grad_out, weights, saved, cosine, sine):
    w_qkv, w_out, gain_a, shift_a, w_gate, w_up, w_down, gain_f, shift_f = weights
    (
        act,
        query_r,
        keys_r,
        values_r,
        log_total,
        context,
        res_a,
        act_f,
        gate_pre,
        up_pre,
        hidden,
        res_f,
    ) = saved
    tokens = act.shape[0]
    width = act.shape[1]
    heads = width // HEAD
    scale = HEAD ** (-0.5)
    unused, pull_f = jax.vjp(
        layer_norm, res_f, gain_f.astype(jnp.float32), shift_f.astype(jnp.float32)
    )
    d_res_f, d_gain_f, d_shift_f = pull_f(grad_out)
    d_branch = d_res_f.astype(jnp.bfloat16)
    g_down = dot_first(hidden, d_branch)
    d_hidden = dot_last(d_branch, w_down)
    sigm = jax.nn.sigmoid(gate_pre)
    d_gate = (d_hidden * up_pre * sigm * (1.0 + gate_pre * (1.0 - sigm))).astype(jnp.bfloat16)
    d_up = (d_hidden * gate_pre * sigm).astype(jnp.bfloat16)
    g_gate = dot_first(act_f, d_gate)
    g_up = dot_first(act_f, d_up)
    d_norm_a = d_res_f + dot_last(d_gate, w_gate) + dot_last(d_up, w_up)
    unused, pull_a = jax.vjp(
        layer_norm, res_a, gain_a.astype(jnp.float32), shift_a.astype(jnp.float32)
    )
    d_res_a, d_gain_a, d_shift_a = pull_a(d_norm_a)
    d_attn = d_res_a.astype(jnp.bfloat16)
    g_out = dot_first(context, d_attn)
    d_context = dot_last(d_attn, w_out).astype(jnp.bfloat16).reshape(tokens, heads, HEAD)
    keys_all, values_all = (
        lax.all_gather(keys_r, "seq", axis=0, tiled=True),
        lax.all_gather(values_r, "seq", axis=0, tiled=True),
    )
    length = keys_all.shape[0]
    keys_all = keys_all.reshape(length, heads, HEAD)
    values_all = values_all.reshape(length, heads, HEAD)
    scores = (
        jnp.einsum("qhd,khd->hqk", query_r, keys_all, preferred_element_type=jnp.float32) * scale
    )
    probs = jnp.exp(scores - log_total)
    d_probs = jnp.einsum("qhd,khd->hqk", d_context, values_all, preferred_element_type=jnp.float32)
    inner = jnp.sum(probs * d_probs, axis=-1, keepdims=True)
    d_scores = (probs * (d_probs - inner)).astype(jnp.bfloat16)
    d_query = (
        jnp.einsum("hqk,khd->qhd", d_scores, keys_all, preferred_element_type=jnp.float32) * scale
    )
    d_keys_all = (
        jnp.einsum("hqk,qhd->khd", d_scores, query_r, preferred_element_type=jnp.float32) * scale
    )
    d_values_all = jnp.einsum(
        "hqk,qhd->khd", probs.astype(jnp.bfloat16), d_context, preferred_element_type=jnp.float32
    )
    d_keys, d_values = (
        lax.psum_scatter(
            d_keys_all.reshape(length, width).astype(jnp.bfloat16),
            "seq",
            scatter_dimension=0,
            tiled=True,
        ).astype(jnp.float32),
        lax.psum_scatter(
            d_values_all.reshape(length, width).astype(jnp.bfloat16),
            "seq",
            scatter_dimension=0,
            tiled=True,
        ).astype(jnp.float32),
    )
    d_query = unrotate(d_query, cosine, sine).reshape(tokens, width)
    d_keys = unrotate(d_keys.reshape(tokens, heads, HEAD), cosine, sine).reshape(tokens, width)
    d_joint = jnp.concatenate([d_query, d_keys, d_values], axis=1).astype(jnp.bfloat16)
    g_qkv = dot_first(act, d_joint)
    grad_in = d_res_a + dot_last(d_joint, w_qkv)
    return (grad_in, (g_qkv, g_out, d_gain_a, d_shift_a, g_gate, g_up, g_down, d_gain_f, d_shift_f))


def per_device(
    inputs,
    cotangent,
    live,
    first_qkv,
    first_out,
    first_gain_a,
    first_shift_a,
    first_gate,
    first_up,
    first_down,
    first_gain_f,
    first_shift_f,
    second_qkv,
    second_out,
    second_gain_a,
    second_shift_a,
    second_gate,
    second_up,
    second_down,
    second_gain_f,
    second_shift_f,
):
    local_sets = (
        (
            first_qkv,
            first_out,
            first_gain_a,
            first_shift_a,
            first_gate,
            first_up,
            first_down,
            first_gain_f,
            first_shift_f,
        ),
        (
            second_qkv,
            second_out,
            second_gain_a,
            second_shift_a,
            second_gate,
            second_up,
            second_down,
            second_gain_f,
            second_shift_f,
        ),
    )
    micro = inputs.shape[0]
    tokens = inputs.shape[2]
    groups = lax.axis_size("dp")
    positions = (lax.axis_index("seq") * tokens + jnp.arange(tokens)).astype(jnp.float32)
    cosine, sine = tables(positions)
    totals = [
        tuple(
            (jnp.zeros((w.shape[0] * groups,) + w.shape[1:], jnp.float32) for w in local_sets[0])
        ),
        tuple(
            (jnp.zeros((w.shape[0] * groups,) + w.shape[1:], jnp.float32) for w in local_sets[1])
        ),
    ]
    results = []
    grads_in = []
    for batch in range(micro):
        flag = live[batch, 0].astype(jnp.float32)
        state = inputs[batch, 0].astype(jnp.float32)
        held = []
        saves = []
        for index in range(2):
            full = lax.all_gather(as_sent(local_sets[index]), "dp", axis=0, tiled=True)
            held.append(full)
            state, saved = forward_layer(state, full, cosine, sine)
            saves.append(saved)
        results.append((state * flag).astype(jnp.bfloat16))
        grad = cotangent[batch, 0].astype(jnp.float32) * flag
        for index in (1, 0):
            full = lax.all_gather(as_sent(local_sets[index]), "dp", axis=0, tiled=True)
            grad, terms = backward_layer(grad, full, saves[index], cosine, sine)
            totals[index] = tuple((old + new for old, new in zip(totals[index], terms)))
        grads_in.append(grad.astype(jnp.bfloat16))
    summed = []
    for index in range(2):
        shares = jax.tree.map(
            lambda part: part.astype(jnp.float32),
            lax.psum_scatter(as_sent(totals[index]), "dp", scatter_dimension=0, tiled=True),
        )
        final = jax.tree.map(
            lambda part: part.astype(jnp.float32), lax.psum(as_sent(shares), "seq")
        )
        summed.extend(final)
    output = jnp.stack(results)[:, None]
    input_grad = jnp.stack(grads_in)[:, None]
    return (output, input_grad) + tuple(summed)


def solution(mesh):
    def device(inputs, cotangent, *rest):
        if fits(mesh) and inputs.shape == (2, 1, TOK, D):
            return shared_device(inputs, cotangent, *rest)
        return per_device(inputs, cotangent, *rest)

    return jax.shard_map(
        device,
        mesh=mesh,
        in_specs=(
            P(None, "dp", "seq", None),
            P(None, "dp", "seq", None),
            P(None, "dp"),
            P("dp", None),
            P("dp", None),
            P("dp"),
            P("dp"),
            P("dp", None),
            P("dp", None),
            P("dp", None),
            P("dp"),
            P("dp"),
            P("dp", None),
            P("dp", None),
            P("dp"),
            P("dp"),
            P("dp", None),
            P("dp", None),
            P("dp", None),
            P("dp"),
            P("dp"),
        ),
        out_specs=(
            P(None, "dp", "seq", None),
            P(None, "dp", "seq", None),
            P("dp", None),
            P("dp", None),
            P("dp"),
            P("dp"),
            P("dp", None),
            P("dp", None),
            P("dp", None),
            P("dp"),
            P("dp"),
            P("dp", None),
            P("dp", None),
            P("dp"),
            P("dp"),
            P("dp", None),
            P("dp", None),
            P("dp", None),
            P("dp"),
            P("dp"),
        ),
        check_vma=False,
    )
```

```python
import functools

import jax
import jax.numpy as jnp
import numpy as np
from jax import lax
from jax.experimental import pallas as pl
from jax.experimental.pallas import tpu as pltpu
from jax.sharding import PartitionSpec as P

HEAD = 64

DP = 4
SQ = 8
TOK = 128
PART = TOK // DP
ROWS = TOK + PART
ALL = DP * ROWS
HALF = 2 * ROWS
D = 768
LEN = SQ * TOK
QB = 256
F32 = jnp.float32
BF16 = jnp.bfloat16
VMEM_LIMIT = 64 * 2**20
MESH = pl.DeviceIdType.MESH


def mm(a, b):
    return lax.dot_general(a, b, (((1,), (0,)), ((), ())), preferred_element_type=F32)


def mm_t(a, b):
    return lax.dot_general(a, b, (((1,), (1,)), ((), ())), preferred_element_type=F32)


def t_mm(a, b):
    return lax.dot_general(a, b, (((0,), (0,)), ((), ())), preferred_element_type=F32)


def low_lanes(shape):
    return lax.rem(lax.broadcasted_iota(jnp.int32, shape, len(shape) - 1), 128) < 64


def swap_halves(x):
    lane = lax.broadcasted_iota(jnp.int32, x.shape, 1)
    return jnp.where(lax.rem(lane, 64) < 32, pltpu.roll(x, 96, 1), pltpu.roll(x, 32, 1))


def flip(x):
    return pltpu.roll(x, 64, 1)


class Links:
    def __init__(self, send, recv, lsem):
        self.send, self.recv, self.used, self.sent, self.slow = send, recv, 0, [], []
        self.lsem, self.locals_used = lsem, 0
        self.d = lax.axis_index("dp")
        self.s = lax.axis_index("seq")
        self.x = self.d // 2
        self.core = lax.rem(self.d, 2)
        self.sib = 2 * self.x + (1 - self.core)
        self.xp = lax.rem(self.d + 2, DP)
        self.diag = lax.rem(self.sib + 2, DP)
        self.z = self.s // 2
        self.y = lax.rem(self.s, 2)
        self.dp_peers = [self.xp, self.diag, self.sib]
        self.seq_peers = [lax.rem(self.s + k, SQ) for k in range(1, SQ)]
        self.yp = (self.d, 2 * self.z + (1 - self.y))
        self.zp = [lax.rem(self.z + k, ZS) for k in range(1, ZS)]
        self.zdev = [(self.d, 2 * p + self.y) for p in self.zp]

    def enter(self):
        peers = [(p, self.s) for p in self.dp_peers] + [(self.d, p) for p in self.seq_peers]
        bar = pltpu.get_barrier_semaphore()
        for p in peers:
            pl.semaphore_signal(bar, inc=1, device_id=p, device_id_type=MESH)
        pl.semaphore_wait(bar, len(peers))

    def describe(self, i, src, dst, to, j=None):
        return pltpu.make_async_remote_copy(
            src_ref=src,
            dst_ref=dst,
            send_sem=self.send.at[i],
            recv_sem=self.recv.at[i if j is None else j],
            device_id=to,
            device_id_type=MESH,
        )

    def local(self, src, dst):
        c = pltpu.make_async_copy(src, dst, self.lsem.at[self.locals_used])
        self.locals_used += 1
        c.start()
        return c

    def copy(self, src, dst, to, slow=False):
        c = self.describe(self.used, src, dst, to)
        self.used += 1
        c.start()
        (self.slow if slow else self.sent).append(c)
        return c

    def settle(self):
        for c in self.sent:
            c.wait_send()
        self.sent = []

    def settle_slow(self):
        for c in self.slow:
            c.wait_send()
        self.slow = []


def span(i, rows):
    return pl.ds(pl.multiple_of(i * rows, 16), rows)


def normalize(res):
    cen = res - jnp.mean(res, axis=-1, keepdims=True)
    rstd = lax.rsqrt(jnp.mean(cen * cen, axis=-1, keepdims=True) + 1e-05)
    return cen * rstd, rstd


def normalize_back(grad, gain, xhat, rstd):
    dn = grad * gain
    return (dn - jnp.mean(dn, axis=-1, keepdims=True) - xhat * jnp.mean(dn * xhat, axis=-1, keepdims=True)) * rstd


def pack_pairs(src, dst):
    half = dst.shape[-1]
    one, two = pl.ds(0, half), pl.ds(half, half)
    keep = low_lanes((TOK, half))
    for e in range(DP):
        dst[e] = src[pl.ds(ROWS * e, TOK), one]
        dst[4, pl.ds(PART * e, PART)] = src[pl.ds(ROWS * e + TOK, PART), one]
        dst[7, pl.ds(PART * e, PART)] = src[pl.ds(ROWS * e + TOK, PART), two]
    for p in range(2):
        a = src[pl.ds(ROWS * 2 * p, TOK), two].astype(F32)
        b = src[pl.ds(ROWS * (2 * p + 1), TOK), two].astype(F32)
        dst[5 + p] = jnp.where(keep, a, b).astype(BF16)


def unpack_pairs(src, dst):
    half = src.shape[-1]
    one, two = pl.ds(0, half), pl.ds(half, half)
    keep = low_lanes((TOK, half))
    third = [src[5].astype(F32), src[6].astype(F32)]
    last = jnp.where(keep, src[7].astype(F32), 0.0).astype(BF16)
    for e in range(DP):
        dst[pl.ds(ROWS * e, TOK), one] = src[e]
        mine = third[e // 2]
        mine = jnp.where(keep, mine, 0.0) if e % 2 == 0 else jnp.where(keep, 0.0, mine)
        dst[pl.ds(ROWS * e, TOK), two] = mine.astype(BF16)
        dst[pl.ds(ROWS * e + TOK, PART), one] = src[4, pl.ds(PART * e, PART)]
        dst[pl.ds(ROWS * e + TOK, PART), two] = last[PART * e : PART * (e + 1)]


class Sums:
    def __init__(self, L, plan, g, ab, f, bufs):
        self.L, self.plan, self.g, self.ab, self.f, self.bufs = L, plan, g, ab, f, bufs
        self.end = L.z // 2
        self.outer = lax.rem(L.z, ZS - 1) == 0
        self.inner = lax.rem(L.z, ZS - 1) != 0
        self.inward = (L.d, 2 * (1 + self.end) + L.y)
        self.outward = (L.d, 2 * (3 * self.end) + L.y)
        self.across = (L.d, 2 * (3 - L.z) + L.y)
        self.outer_sent, self.inner_sent, self.todo = [], [], {}

    def send(self, role, i, j, src, dst, to):
        def make():
            return self.L.describe(i, src(), dst(), to, j)

        make().start()
        role.append(make)

    def send_all(self, i, src, dst, to):
        c = self.L.describe(i, src, dst, to)
        c.start()
        self.L.slow.append(c)

    def got(self, i, ref):
        self.L.describe(i, ref, ref, self.L.yp).wait_recv()

    def start(self, name):
        kind = self.plan[name][4]
        self.todo[name] = (self.direct_steps if kind == "d" else self.chain_steps)(name)
        next(self.todo[name])

    def advance(self, name):
        next(self.todo[name], None)

    def add(self, where, more):
        self.g[where] = (self.g[where].astype(F32) + more[...].astype(F32)).astype(BF16)

    def prepare(self, name):
        at, n, off, width, kind, k0 = self.plan[name][:6]
        i, l = self.L.used, self.L.locals_used
        self.L.used += 11
        self.L.locals_used += 1
        rows = lambda e: pl.ds(pl.multiple_of(e * HR, HR), HR)
        cols = lambda e: pl.ds(pl.multiple_of(e * YC + off, 128), width)
        return i, l, at, pl.ds(at, n), pl.ds(k0, n), rows, cols

    def chain_steps(self, name):
        L, g, f = self.L, self.g, self.f
        i, l, at, r, b, rows, cols = self.prepare(name)
        end, y = self.end, L.y
        k0 = self.plan[name][5]
        zfirst = self.plan[name][4] == "z"
        off, width = self.plan[name][2:4]
        within = pl.ds(off, width)
        half = self.bufs.rh.at[b, :, within] if zfirst else None
        ab = self.ab
        if zfirst:
            piece = lambda e: (r, slice(None), cols(e))
            first, second = self.bufs.zf.at[b, :, within], self.bufs.zs.at[b, :, within]
            spare = self.bufs.zf
            final = (r, rows(y), cols(end))
        else:
            piece = lambda e: (r, rows(e), cols(y))
            first, second = self.bufs.pf.at[b, :, within], self.bufs.ps.at[b, :, within]
            spare = self.bufs.pf
            ry = self.bufs.ry.at[b, :, within]
            final = (r, rows(end), cols(y))

        def across_dp(k):
            p = L.dp_peers[k]
            return L.describe(i + 3 + k, spare.at[k0 + p, pl.ds(0, HR), within], ab.at[at + L.d, :, within], (p, L.s))

        local = lambda: pltpu.make_async_copy(ab.at[r, :, within], f.at[final], L.lsem.at[l])

        if not zfirst:
            self.send_all(i, g.at[r, :, cols(1 - y)], ry, L.yp)
            yield
            self.got(i, ry)
            self.add((r, slice(None), cols(y)), ry)

        @pl.when(self.outer)
        def _():
            self.send(self.outer_sent, i + 1, i + 1, lambda: g.at[piece(1 - end)], lambda: first, self.inward)

        yield

        @pl.when(self.inner)
        def _():
            self.got(i + 1, first)
            self.add(piece(1 - end), first)
            self.send(self.inner_sent, i + 1, i + 2, lambda: g.at[piece(1 - end)], lambda: second, self.across)

        yield

        @pl.when(self.inner)
        def _():
            self.got(i + 2, second)
            self.add(piece(end), second)
            self.send(self.inner_sent, i + 2, i + 2, lambda: g.at[piece(end)], lambda: second, self.outward)

        yield
        if zfirst:

            @pl.when(self.outer)
            def _():
                self.got(i + 2, second)
                self.add(piece(end), second)
                self.send(self.outer_sent, i, i, lambda: g.at[r, rows(1 - y), cols(end)], lambda: half, L.yp)

            yield

        @pl.when(self.outer)
        def _():
            if zfirst:
                self.got(i, half)
                total = g[final].astype(F32) + half[...].astype(F32)
            else:
                self.got(i + 2, second)
                total = g[final].astype(F32) + second[...].astype(F32)
            if at < 12:
                spare[b, pl.ds(0, HR), within] = total.astype(BF16)
                for k in range(DP - 1):
                    across_dp(k).start()
                ab[at + L.d, :, within] = spare[k0 + L.d, pl.ds(0, HR), within]
            else:
                ab[r, :, within] = total.astype(BF16)

        yield

        @pl.when(self.outer)
        def _():
            if at < 12:
                for k in range(DP - 1):
                    across_dp(k).wait()
            self.send(self.outer_sent, i + 6, i + 6, lambda: ab.at[r, :, within], lambda: f.at[final], L.yp if zfirst else self.inward)
            local().start()

        yield
        if zfirst:

            @pl.when(self.outer)
            def _():
                self.got(i + 6, ab.at[r, :, within])
                local().wait()
                self.send(self.outer_sent, i + 9, i + 9, lambda: f.at[piece(end)], lambda: f.at[piece(end)], self.inward)

            yield

        @pl.when(self.inner)
        def _():
            self.got(i + (9 if zfirst else 6), f.at[piece(end)])
            self.send(self.inner_sent, i + 7, i + 7, lambda: f.at[piece(end)], lambda: f.at[piece(end)], self.across)

        yield

        @pl.when(self.inner)
        def _():
            self.got(i + 7, f.at[piece(1 - end)])
            self.send(self.inner_sent, i + 8, i + 8, lambda: f.at[piece(1 - end)], lambda: f.at[piece(1 - end)], self.outward)

        yield

        @pl.when(self.outer)
        def _():
            self.got(i + 8, f.at[piece(1 - end)])
            if not zfirst:
                local().wait()

        if not zfirst:
            whole = f.at[r, :, cols(y)]
            self.send_all(i + 9, whole, whole, L.yp)
            yield
            self.got(i + 9, whole)

    def direct_steps(self, name):
        L, g, f = self.L, self.g, self.f
        i, l, at, r, b, rows, cols = self.prepare(name)
        n, off, width = self.plan[name][1:4]
        mine = cols(L.y)
        within = pl.ds(off, width)
        ry = self.bufs.ry.at[b, :, within]
        quarter = lambda z: pl.ds(pl.multiple_of(z * (HR // 2), HR // 2), HR // 2)
        own = (r, quarter(L.z), mine)
        k1 = self.plan[name][6]
        c = pl.ds(k1, n)
        got, out, ab = self.bufs.qz, self.bufs.qo, self.bufs.qa
        self.send_all(i, g.at[r, :, cols(1 - L.y)], ry, L.yp)
        yield
        self.got(i, ry)
        self.add((r, slice(None), mine), ry)
        for k in range(ZS - 1):
            self.send_all(i + 1 + k, g.at[r, quarter(L.zp[k]), mine], got.at[k, c, :, within], L.zdev[k])
        yield
        total = g[own].astype(F32)
        for k in range(ZS - 1):
            self.got(i + 1 + k, got.at[k, c, :, within])
            total = total + got[k, c, :, within].astype(F32)
        if at < 12:
            out[c, :, within] = total.astype(BF16)
            for k, p in enumerate(L.dp_peers):
                self.send_all(i + 4 + k, out.at[k1 + p, :, within], ab.at[k1 + L.d, :, within], (p, L.s))
            ab[k1 + L.d, :, within] = out[k1 + L.d, :, within]
            yield
            for k in range(DP - 1):
                self.got(i + 4 + k, ab.at[k1, :, within])
        else:
            ab[c, :, within] = total.astype(BF16)
        local = pltpu.make_async_copy(ab.at[c, :, within], f.at[own], L.lsem.at[l])
        local.start()
        for k in range(ZS - 1):
            self.send_all(i + 7 + k, ab.at[c, :, within], f.at[own], L.zdev[k])
        yield
        local.wait()
        for k in range(ZS - 1):
            self.got(i + 7 + k, f.at[own])
        whole = f.at[r, :, mine]
        self.send_all(i + 10, whole, whole, L.yp)
        yield
        self.got(i + 10, whole)

    def settle(self):
        @pl.when(self.outer)
        def _():
            for make in self.outer_sent:
                make().wait_send()

        @pl.when(self.inner)
        def _():
            for make in self.inner_sent:
                make().wait_send()


class Stage:
    def __init__(self, buf, sem):
        self.buf, self.sem, self.count, self.open = buf, sem, 0, {}

    def slot(self):
        i = self.count % STAGES
        if i in self.open:
            self.open.pop(i).wait()
        return self.buf.at[i]

    def go(self, dst):
        i = self.count % STAGES
        c = pltpu.make_async_copy(self.buf.at[i], dst, self.sem.at[i])
        c.start()
        self.open[i] = c
        self.count += 1

    def settle(self):
        for c in self.open.values():
            c.wait()


def widen_kernel(f0, f1, rows_out, rows_in, *refs):
    outs, (o_out, o_in, buf, stage_buf, in_sem, out_sem) = refs[:10], refs[10:]
    stage = Stage(stage_buf, out_sem)
    moves = [
        pltpu.make_async_copy(rows_out, o_out, in_sem.at[10]),
        pltpu.make_async_copy(rows_in, o_in, in_sem.at[11]),
    ]
    for c in moves:
        c.start()
    keep = low_lanes((QR, 128))
    loads = {}
    for l, f in ((0, f0), (1, f1)):
        for k, (at, n) in enumerate(CHUNKS.values()):
            c = pltpu.make_async_copy(f.at[pl.ds(at, n)], buf.at[l, pl.ds(at, n)], in_sem.at[5 * l + k])
            c.start()
            loads[5 * l + k] = c
    for l in range(2):
        o_qkv, o_out, o_gate, o_up, o_down = outs[5 * l : 5 * l + 5]
        g = buf.at[l]
        for k, (name, (at, n)) in enumerate(CHUNKS.items()):
            loads[5 * l + k].wait()
            for i in range(3 if name == "qkv" else n):
                st = stage.slot()
                if name == "qkv":
                    one, two = pl.ds(128 * i, 128), pl.ds(384 + 128 * i, 128)
                    for a in range(2):
                        po = flip(g[2 * a + 1, :, one].astype(F32))
                        te, to = g[2 * a, :, two].astype(F32), g[2 * a + 1, :, two].astype(F32)
                        st[:, pl.ds(384 * a, 128)] = g[2 * a, :, one].astype(F32)
                        st[:, pl.ds(384 * a + 128, 128)] = jnp.where(keep, te + flip(te), po)
                        st[:, pl.ds(384 * a + 256, 128)] = jnp.where(keep, po, to + flip(to))
                    dst = o_qkv.at[:, pl.ds(D * i, D)]
                else:
                    st[...] = g[at + i].astype(F32)
                    if name == "out":
                        dst = o_out
                    elif name == "down":
                        dst = o_down.at[pl.ds(QR * i, QR)]
                    else:
                        dst = (o_gate if name == "gate" else o_up).at[:, pl.ds(D * i, D)]
                stage.go(dst)
    stage.settle()
    for c in moves:
        c.wait()


CHUNKS = {"qkv": (0, 4), "gate": (4, 4), "up": (8, 4), "down": (12, 4), "out": (16, 1)}
BLOCKS = 17
ZS = 4
QR = D // DP
HR = QR // 2
YC = D // 2
PLAN = [
    {
        "d": (12, 4, 0, 256, "y", 0, 0),
        "D": (12, 4, 256, 128, "y", 0, 0),
        "g": (4, 4, 0, 256, "z", 0, 0),
        "G": (4, 4, 256, 128, "z", 0, 0),
        "u": (8, 4, 0, 256, "y", 4, 0),
        "U": (8, 4, 256, 128, "y", 4, 0),
        "o": (16, 1, 0, YC, "y", 8, 0),
        "q": (0, 4, 0, 256, "d", 9, 0),
        "r": (0, 4, 256, 128, "d", 9, 0),
    },
    {
        "d": (12, 4, 0, 256, "d", 12, 12),
        "D": (12, 4, 256, 128, "d", 12, 12),
        "g": (4, 4, 0, 256, "d", 4, 4),
        "G": (4, 4, 256, 128, "d", 4, 4),
        "u": (8, 4, 0, 256, "d", 8, 8),
        "U": (8, 4, 256, 128, "d", 8, 8),
        "o": (16, 1, 0, YC, "d", 16, 16),
        "q": (0, 4, 0, 256, "d", 0, 0),
        "r": (0, 4, 256, 128, "d", 0, 0),
    },
]
STAGES = 8
SEMS = 480

INS = ["inp", "cot", "aux", "wq0", "wg0", "wu0", "wo0", "wd0", "wq1", "wg1", "wu1", "wo1", "wd1", "cosf", "sinf"]
INS_ANY = {"wq0", "wg0", "wu0", "wd0", "wq1", "wg1", "wu1", "wd1"}
GRADS = [((QR, 3 * D), F32), ((QR, D), F32), ((QR, DP * D), F32), ((QR, DP * D), F32), ((D, D), F32)]
BIG = ((ALL, D), BF16)
OUTS = [("out", ((2, TOK, D), BF16)), ("gin", ((2, TOK, D), BF16)), ("vsum", ((8, D), F32))]
OUTS_ANY = [("fs" + str(i), ((BLOCKS, QR, D), BF16)) for i in range(2)] + [("st" + str(i), BIG) for i in range(5)] + [("sx0", ((ROWS, D), F32)), ("sx1", ((ROWS, D), F32)), ("sx2", ((LEN, 128), F32))]
TALL = ((LEN, 128), BF16)
SCRATCH = (
    [
        (n + str(l), s)
        for l in range(2)
        for n, s in [
            ("qkv", ((LEN, 384), BF16)),
            ("lse", ((8, LEN), F32)),
            ("ce", ((ALL, 256), BF16)),
            ("ra", ((ROWS, 128), F32)),
            ("rf", ((ROWS, 128), F32)),
            ("wqg", ((D, D), BF16)),
            ("wgg", ((D, D), BF16)),
            ("wug", ((D, D), BF16)),
            ("wog", ((256, D), BF16)),
            ("g", ((BLOCKS, QR, D), BF16)),
            ("ry", ((13 + 4 * l, QR, YC), BF16)),
            ("qz", ((ZS - 1, 4 + 13 * l, HR // 2, YC), BF16)),
            ("qo", ((4 + 13 * l, HR // 2, YC), BF16)),
            ("qa", ((4 + 13 * l, HR // 2, YC), BF16)),
        ]
    ]
    + [
        ("x", BIG),
        ("wd", ((D, D), BF16)),
        ("xa", ((ROWS, D), F32)),
        ("xf", ((ROWS, D), F32)),
        ("ctx", ((LEN, 128), F32)),
        ("actf", BIG),
        ("gp", BIG),
        ("up", BIG),
        ("hid", BIG),
        ("part", ((ALL, D), F32)),
        ("ta", BIG),
        ("tb", BIG),
        ("db", BIG),
        ("dsb", BIG),
        ("sb", ((SQ, TOK, 384), BF16)),
        ("sc", ((SQ, TOK, 128), BF16)),
        ("rx", ((SQ, TOK, 384), BF16)),
        ("rc", ((SQ, TOK, 128), BF16)),
        ("dc", TALL),
        ("cb", TALL),
        ("kz", ((2, LEN, 128), BF16)),
        ("vz", ((2, LEN, 128), BF16)),
        ("kt", ((2, 128, LEN), BF16)),
        ("et", ((128, LEN), F32)),
        ("cz", ((2, LEN, 128), BF16)),
        ("inner", ((8, LEN), F32)),
        ("hres", ((ROWS, D), F32)),
        ("gres", ((ROWS, D), F32)),
        ("nv", ((8, D), F32)),
        ("auxs", ((DP, 16, 256), F32)),
        ("cbuf", ((DP, 2, PART, D), BF16)),
        ("loa", ((2, DP, PART, D), BF16)),
        ("los", ((2, PART, D), BF16)),
        ("ab", ((BLOCKS, HR, YC), BF16)),
        ("rh", ((4, HR, YC), BF16)),
        ("pf", ((9, HR, YC), BF16)),
        ("ps", ((9, HR, YC), BF16)),
        ("zf", ((4, QR, YC), BF16)),
        ("zs", ((4, QR, YC), BF16)),
        ("va", ((8, D), F32)),
        ("vb", ((8, D), F32)),
        ("vc", ((8, D), F32)),
        ("vd", ((8, D), F32)),
        ("vy", ((8, D), F32)),
        ("vz3", ((ZS - 1, 8, D), F32)),
        ("vs", ((8, D), F32)),
        ("vx", ((8, D), F32)),
    ]
    + [(n + k, s) for k in "af" for n, s in [("snd", ((2, ROWS, D), BF16)), ("got", ((2, ROWS, D), BF16)), ("mid", ((ROWS, D), BF16)), ("fin", ((ROWS, D), BF16))]]
)


class Named:
    pass


def whole_kernel(*refs):
    R = Named()
    names = INS + [n for n, _ in OUTS + OUTS_ANY + SCRATCH]
    for n, r in zip(names, refs):
        setattr(R, n, r)
    L = Links(*refs[len(names) :])
    d, s = L.d, L.s
    own = pl.ds(pl.multiple_of(d * ROWS, 32), ROWS)
    tok = pl.ds(pl.multiple_of(s * TOK, TOK), TOK)

    def at_layer(n, l):
        return getattr(R, n + str(l))

    def chip(c):
        return pl.ds(pl.multiple_of(c * HALF, 32), HALF)

    local = L.local

    def rows_at(ref, i):
        return ref.at[span(i, ROWS)]

    def input_at(ref, i):
        return ref.at[pl.ds(2 * i, 2), pl.ds(0, TOK)]

    def gather_begin(ref, at=rows_at):
        far = L.copy(at(ref, d), at(ref, d), (L.xp, s))
        near = L.copy(at(ref, d), at(ref, d), (L.sib, s))
        return near, far

    def gather_forward(ref, far, at=rows_at):
        far.wait_recv()
        return L.copy(at(ref, L.xp), at(ref, L.xp), (L.sib, s))

    part = R.part

    def reduce_chip(k, i):
        snd, got = getattr(R, "snd" + k), getattr(R, "got" + k)
        snd[i] = part[span(L.diag if i else L.sib, ROWS)].astype(BF16)
        return L.copy(snd.at[i], got.at[i], (L.sib, s))

    def reduce_cross(k, c_other):
        got, mid, fin = getattr(R, "got" + k), getattr(R, "mid" + k), getattr(R, "fin" + k)
        c_other.wait_recv()
        mid[...] = (part[span(L.xp, ROWS)] + got[1].astype(F32)).astype(BF16)
        return L.copy(mid, fin, (L.xp, s))

    def reduce_end(k, c_own, c_cross):
        got, fin = getattr(R, "got" + k), getattr(R, "fin" + k)
        c_own.wait_recv()
        c_cross.wait_recv()
        return part[own] + got[0].astype(F32) + fin[...].astype(F32)

    lqs = [
        [local(getattr(R, "wq" + str(l)).at[:, pl.ds(D * t, D)], R.g1.at[8 + 3 * l + t]) for t in range(3)]
        for l in range(2)
    ]
    mycols = pl.ds(pl.multiple_of(d * D, D), D)
    mydep = pl.ds(pl.multiple_of(d * QR, 64), QR)
    lws = []
    for l in range(2):
        for n in "gu":
            lws.append(local(getattr(R, "w" + n + str(l)).at[:, mycols], at_layer("w" + n + "g", l).at[mydep]))
    lws.append(local(R.wd0, R.wd))
    inb = R.g0
    inb[pl.ds(2 * d, 2), pl.ds(0, TOK)] = R.inp[...]
    R.auxs[d] = R.aux[...]
    L.enter()
    small = [L.copy(R.aux, R.auxs.at[d], (p, s)) for p in L.dp_peers]

    hq = QR // 2
    mine_half = L.y * hq

    def arrange_qkv(l):
        for c in lqs[l]:
            c.wait()
        keep = low_lanes((QR, 128))
        for t in range(3):
            for a in range(2):
                t0, t1, t2 = [R.g1[8 + 3 * l + t, :, pl.ds(384 * a + 128 * i, 128)].astype(F32) for i in range(3)]
                f1, f2 = flip(t1), flip(t2)
                for p, one, two in (
                    (2 * a, t0, jnp.where(keep, t1, f1)),
                    (2 * a + 1, jnp.where(keep, f1, f2), jnp.where(keep, f2, t2)),
                ):
                    R.g1[4 * l + p, :, pl.ds(128 * t, 128)] = one.astype(BF16)
                    R.g1[4 * l + p, :, pl.ds(384 + 128 * t, 128)] = two.astype(BF16)

    def share_qkv(l):
        w = at_layer("wqg", l)
        far = []
        for p in (L.xp, L.diag):
            src = R.g1.at[4 * l + p, pl.ds(pl.multiple_of(mine_half, 32), hq)]
            far.append(L.copy(src, w.at[pl.ds(pl.multiple_of(d * QR + mine_half, 32), hq)], (p, s), True))
        near = L.copy(R.g1.at[4 * l + L.sib], w.at[mydep], (L.sib, s), True)
        w[mydep] = R.g1[4 * l + d]
        return [(w, far, near)]

    def share_ff(l):
        res = []
        for n in "gu":
            w, g = getattr(R, "w" + n + str(l)), at_layer("w" + n + "g", l)
            far = []
            half = pl.ds(pl.multiple_of(mine_half, 32), hq)
            for p in (L.xp, L.diag):
                src = w.at[half, pl.ds(pl.multiple_of(p * D, D), D)]
                far.append(L.copy(src, g.at[pl.ds(pl.multiple_of(d * QR + mine_half, 32), hq)], (p, s), True))
            near = L.copy(w.at[:, pl.ds(pl.multiple_of(L.sib * D, D), D)], g.at[mydep], (L.sib, s), True)
            res.append((g, far, near))
        return res

    def pass_on(shares):
        res = []
        for w, far, near in shares:
            for c, p in zip(far, (L.xp, L.diag)):
                c.wait_recv()
                o = pl.ds(pl.multiple_of(p * QR + mine_half, 32), hq)
                res.append(L.copy(w.at[o], w.at[o], L.yp, True))
            res.append(near)
        return res

    arrange_qkv(0)
    sq = share_qkv(0)
    near, far = gather_begin(inb, input_at)
    for l in range(2):
        wo, wog = getattr(R, "wo" + str(l)), at_layer("wog", l)
        wog[pl.ds(0, QR)] = wo[...]
        wog[pl.ds(QR, 64)] = wo[pl.ds(128, 64)]
    arrange_qkv(1)
    for c in small:
        c.wait_recv()
    keep8 = low_lanes((8, 128))
    for a in range(2):
        e, o = R.auxs.at[2 * a], R.auxs.at[2 * a + 1]
        eight = pl.ds(0, 8)
        lo, hi = pl.ds(0, 128), pl.ds(128, 128)
        po = flip(o[eight, lo])
        R.nv[:, pl.ds(384 * a, 128)] = e[eight, lo]
        R.nv[:, pl.ds(384 * a + 128, 128)] = jnp.where(keep8, e[eight, hi], po)
        R.nv[:, pl.ds(384 * a + 256, 128)] = jnp.where(keep8, po, flip(o[eight, hi]))

    def flag(j, m):
        v = R.auxs[j, 8 + m : 9 + m]
        return jnp.concatenate([v, v, v], axis=1)

    f0 = flag(0, 0) * flag(1, 0) * flag(2, 0) * flag(3, 0)
    f1 = 1.0 - f0
    lone_flag = [f0 * flag(j, 1) + f1 * flag(j, 0) for j in range(DP)]
    lone_mine = f0 * flag(d, 1) + f1 * flag(d, 0)

    shares = pass_on(sq)
    fwd = gather_forward(inb, far, input_at)
    near.wait_recv()
    fwd.wait_recv()
    lone = None
    for j in range(DP):
        a = inb[2 * j, pl.ds(0, TOK)].astype(F32)
        b = inb[2 * j + 1, pl.ds(0, TOK)].astype(F32)
        R.x[pl.ds(ROWS * j, TOK)] = (f0 * a + f1 * b).astype(BF16)
        term = lone_flag[j] * (f0 * b + f1 * a)
        lone = term if lone is None else lone + term
    lone = lone.astype(BF16)
    for j in range(DP):
        R.x[pl.ds(ROWS * j + TOK, PART)] = lone[PART * j : PART * (j + 1)]
    R.hres[...] = R.x[own].astype(F32)
    for c in shares:
        c.wait_recv()

    later = {}
    stash = []

    def forward(l):
        x = R.x
        ctx = R.ctx
        qkv, lse, ce = [at_layer(n, l) for n in ("qkv", "lse", "ce")]
        wq, wg, wu, wo = [at_layer(n, l) for n in ("wqg", "wgg", "wug", "wog")]
        wd = R.wd
        qx = R.ta

        def project(c):
            rows = chip(c)
            a = x[rows]
            y = [mm(a, wq[:, pl.ds(256 * t, 256)]) for t in range(3)]
            for b in range(2):
                j = 2 * c + b
                lone_at = pl.ds(pl.multiple_of(s * TOK + j * PART, PART), PART)
                co = jnp.concatenate([R.cosf[tok], R.cosf[lone_at]], axis=0)
                si = jnp.concatenate([R.sinf[tok], R.sinf[lone_at]], axis=0)
                for t in range(6):
                    v = y[t // 2][ROWS * b : ROWS * (b + 1), 128 * (t % 2) : 128 * (t % 2 + 1)]
                    if t % 3 != 2:
                        v = v * co + swap_halves(v) * si
                    if t % 3 == 0:
                        v = v * (HEAD**-0.5)
                    qx[span(j, ROWS), pl.ds(128 * t, 128)] = v.astype(BF16)

        if l == 0:
            project(0)
            project(1)
            keep_x = local(x, R.st4)
        else:
            x[own] = R.hres[...].astype(BF16)
            near, far = gather_begin(x)
            near.wait_recv()
            project(L.x)
            fwd = gather_forward(x, far)
            fwd.wait_recv()
            project(1 - L.x)

        for c in stash:
            c.wait()
        del stash[:]
        pack_pairs(qx, R.sb)
        qkv[tok] = R.sb[s]
        qc = [L.copy(R.sb.at[p], qkv.at[tok], (d, p)) for p in L.seq_peers]
        cc = []
        ff = share_ff(l)
        if l == 0:
            for p in L.dp_peers:
                r = pl.ds(pl.multiple_of(p * PART, PART), PART)
                cc.append(L.copy(R.cot.at[:, r, :], R.cbuf.at[d], (p, s)))
            R.cbuf[d] = R.cot[:, pl.ds(pl.multiple_of(d * PART, PART), PART), :]
        for c in qc:
            c.wait_recv()

        keep = low_lanes((LEN, 128))
        k = qkv[:, pl.ds(128, 128)].astype(F32)
        R.kz[0] = jnp.where(keep, k, 0.0).astype(BF16)
        R.kz[1] = jnp.where(keep, 0.0, k).astype(BF16)
        base = L.used
        L.used += SQ

        def back(p, i):
            r = pl.ds(pl.multiple_of(p * TOK, TOK), TOK)
            return L.describe(i, R.cb.at[r], R.rc.at[s], (d, p))

        @pl.loop(0, LEN // QB)
        def _(i):
            at = pl.ds(pl.multiple_of(i * QB, QB), QB)
            q = qkv[at, pl.ds(0, 128)]
            outs, logs = [], []
            for j in range(2):
                sc = mm_t(q, R.kz[j])
                top = jnp.max(sc, axis=-1, keepdims=True)
                ex = jnp.exp(sc - top)
                tot = jnp.sum(ex, axis=-1, keepdims=True)
                o = mm(ex.astype(BF16), qkv[:, pl.ds(256, 128)])
                outs.append(o / tot)
                logs.append(jnp.broadcast_to(top + jnp.log(tot), (QB, 128)))
            pick = low_lanes((QB, 128))
            c = jnp.where(pick, outs[0], outs[1])
            ctx[at] = c
            R.et[:, at] = jnp.where(pick, logs[0], logs[1]).T
            R.cb[at] = c.astype(BF16)
            for h in range(QB // TOK):
                p = (QB // TOK) * i + h
                k = lax.rem(p - s + SQ, SQ)

                @pl.when(k != 0)
                def _():
                    back(p, base + k).start()

        lse[0:1] = R.et[0:1]
        lse[1:2] = R.et[64:65]
        R.rc[s] = R.cb[tok]
        ffp = pass_on(ff)
        if l == 0:
            later["q"] = share_qkv(1)
            for c in cc:
                c.wait_recv()
            a = R.cot[0].astype(F32)
            b = R.cot[1].astype(F32)
            R.gres[pl.ds(0, TOK)] = f0 * a + f1 * b
            lone = None
            for j in range(DP):
                term = lone_flag[j] * (f0 * R.cbuf[j, 1].astype(F32) + f1 * R.cbuf[j, 0].astype(F32))
                lone = term if lone is None else lone + term
            R.gres[pl.ds(TOK, PART)] = lone
        for k in range(1, SQ):
            back(L.seq_peers[k - 1], base + k).wait_recv()
        unpack_pairs(R.rc, ce)

        for c in (1 - L.x, L.x):
            a = ce[chip(c)]
            for t in range(3):
                cs = pl.ds(256 * t, 256)
                part[chip(c), cs] = mm(a, wo[:, cs])
        for k in range(1, SQ):
            back(L.seq_peers[k - 1], base + k).wait_send()
        L.settle()
        if l == 0:
            keep_x.wait()
        c_other = reduce_chip("a", 1)
        c_own = reduce_chip("a", 0)
        c_cross = reduce_cross("a", c_other)
        res = R.hres[...] + reduce_end("a", c_own, c_cross)
        n = 4 * l
        xhat, rstd = normalize(res)
        norm_a = xhat * R.nv[n : n + 1] + R.nv[n + 1 : n + 2]
        R.actf[own] = norm_a.astype(BF16)
        near, far = gather_begin(R.actf)
        R.hres[...] = norm_a
        R.xa[...] = xhat
        at_layer("ra", l)[...] = jnp.broadcast_to(rstd, (ROWS, 128))
        if l == 0:
            for c in lws:
                c.wait()
        for c in ffp:
            c.wait_recv()

        def feed(rows):
            a = R.actf[rows]
            for t in range(3):
                cs = pl.ds(256 * t, 256)
                gp = mm(a, wg[:, cs])
                up = mm(a, wu[:, cs])
                R.gp[rows, cs] = gp.astype(BF16)
                R.up[rows, cs] = up.astype(BF16)
                R.hid[rows, cs] = (gp * jax.nn.sigmoid(gp) * up).astype(BF16)
            h = R.hid[rows]
            for t in range(3):
                cs = pl.ds(256 * t, 256)
                part[rows, cs] = mm(h, wd[:, cs])

        near.wait_recv()
        feed(chip(L.x))
        L.settle()
        c_own = reduce_chip("f", 0)
        fwd = gather_forward(R.actf, far)
        fwd.wait_recv()
        feed(chip(1 - L.x))
        c_other = reduce_chip("f", 1)
        c_cross = reduce_cross("f", c_other)
        if l == 0:
            later["q"] = pass_on(later["q"])
            for i, r in enumerate((R.actf, R.gp, R.up, R.hid)):
                stash.append(local(r, getattr(R, "st" + str(i))))
            stash.append(local(R.xa, R.sx0))
            stash.append(local(R.ctx, R.sx2))
            stash.append(local(R.wd1, R.wd))
            for c in later["q"]:
                c.wait_recv()
        res = R.hres[...] + reduce_end("f", c_own, c_cross)
        xhat, rstd = normalize(res)
        h = xhat * R.nv[n + 2 : n + 3] + R.nv[n + 3 : n + 4]
        R.xf[...] = xhat
        if l == 0:
            stash.append(local(R.xf, R.sx1))
        at_layer("rf", l)[...] = jnp.broadcast_to(rstd, (ROWS, 128))
        R.hres[...] = h
        L.settle()

    def lone_begin(k, rows):
        R.los[k] = rows.astype(BF16)
        R.loa[k, d] = rows.astype(BF16)
        return [L.copy(R.los.at[k], R.loa.at[k, d], (p, s)) for p in L.dp_peers]

    def lone_end(k, copies, whole, dst):
        for c in copies:
            c.wait_recv()
        lone = lone_mine * R.loa[k].reshape(TOK, D).astype(F32)
        dst[0] = (f0 * whole + f1 * lone).astype(BF16)
        dst[1] = (f1 * whole + f0 * lone).astype(BF16)

    forward(0)
    forward(1)
    lone_out = lone_begin(0, R.hres[pl.ds(TOK, PART)])


    def tick(codes):
        for c in codes:
            total = sums[int(c[1])]
            total.advance(c[0]) if c[0] in total.todo else total.start(c[0])

    sums = []
    for l in range(2):
        bufs = Named()
        for n in ("rh", "pf", "ps", "zf", "zs"):
            setattr(bufs, n, getattr(R, n))
        for n in ("ry", "qz", "qo", "qa"):
            setattr(bufs, n, at_layer(n, l))
        sums.append(Sums(L, PLAN[l], at_layer("g", l), R.ab, at_layer("fs", l), bufs))
    R.va[...] = jnp.zeros_like(R.va)

    def backward(l, ticks):
        x = R.x
        ctx = R.ctx
        qkv, lse, ce = [at_layer(n, l) for n in ("qkv", "lse", "ce")]
        wq, wg, wu, wo = [at_layer(n, l) for n in ("wqg", "wgg", "wug", "wog")]
        wd = R.wd
        g, n, total = at_layer("g", l), 4 * l, sums[l]

        def grad_of(name, a, b):
            at, c = CHUNKS[name]
            for t in range(3):
                cs = pl.ds(256 * t, 256)
                g[pl.ds(at, c), :, cs] = t_mm(a[...], b[:, cs]).astype(BF16).reshape(c, QR, 256)
            for k in PLAN[l]:
                if PLAN[l][k][0] == at and k + str(l) not in LATER:
                    total.start(k)

        grad = R.gres[...]
        xhat = R.xf[...]
        d_res_f = normalize_back(grad, R.nv[n + 2 : n + 3], xhat, at_layer("rf", l)[:, 0:1])
        R.db[own] = d_res_f.astype(BF16)
        near, far = gather_begin(R.db)
        R.va[n + 2 : n + 3] = jnp.sum(grad * xhat, axis=0, keepdims=True)
        R.va[n + 3 : n + 4] = jnp.sum(grad, axis=0, keepdims=True)
        R.gres[...] = d_res_f
        tick(ticks.get(0, ()))

        def feed(rows):
            a = R.db[rows]
            for t in range(3):
                cs = pl.ds(256 * t, 256)
                dh = mm_t(a, wd[cs])
                gv, uv = R.gp[rows, cs].astype(F32), R.up[rows, cs].astype(F32)
                sig = jax.nn.sigmoid(gv)
                R.ta[rows, cs] = (dh * uv * sig * (1.0 + gv * (1.0 - sig))).astype(BF16)
                R.tb[rows, cs] = (dh * gv * sig).astype(BF16)
            dgv, duv = R.ta[rows], R.tb[rows]
            for t in range(3):
                cs = pl.ds(256 * t, 256)
                part[rows, cs] = mm_t(dgv, wg[cs]) + mm_t(duv, wu[cs])

        near.wait_recv()
        feed(chip(L.x))
        L.settle()
        c_own = reduce_chip("f", 0)
        fwd = gather_forward(R.db, far)
        fwd.wait_recv()
        feed(chip(1 - L.x))
        c_other = reduce_chip("f", 1)
        c_cross = reduce_cross("f", c_other)
        grad_of("down", R.hid, R.db)
        grad_of("gate", R.actf, R.ta)
        grad_of("up", R.actf, R.tb)
        tick(ticks.get(1, ()))
        d_norm = R.gres[...] + reduce_end("f", c_own, c_cross)
        L.settle()
        xhat = R.xa[...]
        d_res_a = normalize_back(d_norm, R.nv[n : n + 1], xhat, at_layer("ra", l)[:, 0:1])
        R.dsb[own] = d_res_a.astype(BF16)
        near, far = gather_begin(R.dsb)
        R.va[n : n + 1] = jnp.sum(d_norm * xhat, axis=0, keepdims=True)
        R.va[n + 1 : n + 2] = jnp.sum(d_norm, axis=0, keepdims=True)
        R.gres[...] = d_res_a
        tick(ticks.get(2, ()))
        reload = []
        if l == 1:
            for i, r in enumerate((R.actf, R.gp, R.up, R.hid)):
                reload.append(local(getattr(R, "st" + str(i)), r))
            reload.append(local(R.sx0, R.xa))
            reload.append(local(R.sx1, R.xf))
            reload.append(local(R.wd0, R.wd))
        fwd = gather_forward(R.dsb, far)
        near.wait_recv()
        fwd.wait_recv()
        R.ta[:, pl.ds(0, 256)] = mm_t(R.dsb[...], wo[...]).astype(BF16)
        pack_pairs(R.ta.at[:, pl.ds(0, 256)], R.sc)
        R.dc[tok] = R.sc[s]
        qc = [L.copy(R.sc.at[p], R.dc.at[tok], (d, p)) for p in L.seq_peers]

        g_out = t_mm(ce[...], R.dsb[...])
        o = CHUNKS["out"][0]
        g[o, pl.ds(0, 128)] = g_out[0:128].astype(BF16)
        g[o, pl.ds(128, 64)] = (g_out[128:192] + g_out[192:256]).astype(BF16)
        total.start("o")
        keep = low_lanes((LEN, 128))
        k = qkv[:, pl.ds(128, 128)].astype(F32)
        k0, k1 = jnp.where(keep, k, 0.0), jnp.where(keep, 0.0, k)
        R.kz[0] = k0.astype(BF16)
        R.kz[1] = k1.astype(BF16)
        R.kt[0] = k0.T.astype(BF16)
        R.kt[1] = k1.T.astype(BF16)
        q = qkv[:, pl.ds(0, 128)].astype(F32)
        R.vz[0] = jnp.where(keep, q, 0.0).astype(BF16)
        R.vz[1] = jnp.where(keep, 0.0, q).astype(BF16)
        tick(ticks.get(3, ()))
        for c in qc:
            c.wait_recv()
        tick(ticks.get(7, ()))
        g2 = R.dc[...].astype(F32)
        et = (g2 * ctx[...]).T
        R.inner[0:1] = jnp.sum(et[0:64], axis=0, keepdims=True)
        R.inner[1:2] = jnp.sum(et[64:128], axis=0, keepdims=True)
        R.cz[0] = jnp.where(keep, g2, 0.0).astype(BF16)
        R.cz[1] = jnp.where(keep, 0.0, g2).astype(BF16)
        if l == 1:
            reload.append(local(R.sx2, ctx))
        R.et[...] = jnp.zeros_like(R.et)
        base = L.used
        L.used += SQ

        def unrotate(v, co, si):
            return v * co - swap_halves(v) * si

        kv = pl.ds(128, 256)

        def back(p, i):
            return L.describe(i, R.sb.at[p, :, kv], R.rx.at[s, :, kv], (d, p))

        @pl.loop(0, LEN // QB)
        def _(i):
            at = pl.ds(pl.multiple_of(i * QB, QB), QB)
            v = qkv[at, pl.ds(256, 128)]
            vf = v.astype(F32)
            pick = low_lanes((QB, 128))
            dk, dv = None, None
            for j in range(2):
                vz = (jnp.where(pick, vf, 0.0) if j == 0 else jnp.where(pick, 0.0, vf)).astype(BF16)
                pr = jnp.exp(mm_t(R.kz[j, at], qkv[:, pl.ds(0, 128)]) - lse[pl.ds(j, 1)])
                dp = mm_t(vz, R.dc[...])
                ds = (pr * (dp - R.inner[pl.ds(j, 1)])).astype(BF16)
                a = mm(pr.astype(BF16), R.cz[j])
                b = mm(ds, R.vz[j])
                dv = a if dv is None else dv + a
                dk = b if dk is None else dk + b
                R.et[...] += mm(R.kt[j, :, at], ds)
            dk = unrotate(dk, R.cosf[at], R.sinf[at]).astype(BF16)
            dv = dv.astype(BF16)
            for h in range(QB // TOK):
                p = (QB // TOK) * i + h
                R.sb[p, :, pl.ds(128, 128)] = dk[TOK * h : TOK * (h + 1)]
                R.sb[p, :, pl.ds(256, 128)] = dv[TOK * h : TOK * (h + 1)]
                k = lax.rem(p - s + SQ, SQ)

                @pl.when(k != 0)
                def _():
                    back(p, base + k).start()

        dq = unrotate(R.et[...].T * (HEAD**-0.5), R.cosf[...], R.sinf[...])
        for p in range(SQ):
            R.sb[p, :, pl.ds(0, 128)] = dq[TOK * p : TOK * (p + 1)].astype(BF16)
        qs = pl.ds(0, 128)
        bc = [L.copy(R.sb.at[p, :, qs], R.rx.at[s, :, qs], (d, p)) for p in L.seq_peers]
        R.rx[s] = R.sb[s]
        tick(ticks.get(4, ()))
        for c in bc:
            c.wait_recv()
        for k in range(1, SQ):
            c = back(L.seq_peers[k - 1], base + k)
            c.wait_recv()
            c.wait_send()
        tick(ticks.get(5, ()))
        unpack_pairs(R.rx, R.tb)
        for c in (1 - L.x, L.x):
            a = R.tb[chip(c)]
            for t in range(3):
                cs = pl.ds(256 * t, 256)
                part[chip(c), cs] = mm_t(a, wq[cs])
        L.settle()
        c_other = reduce_chip("a", 1)
        c_own = reduce_chip("a", 0)
        c_cross = reduce_cross("a", c_other)
        grad_of("qkv", x, R.tb)
        if l == 1:
            reload.append(local(R.st4, x))
        tick(ticks.get(6, ()))
        R.gres[...] = R.gres[...] + reduce_end("a", c_own, c_cross)
        L.settle()
        for c in reload:
            c.wait()

    L.settle_slow()
    backward(1, TICKS[0])
    lone_end(0, lone_out, R.hres[pl.ds(0, TOK)], R.out)
    backward(0, TICKS[1])
    lone_in = lone_begin(1, R.gres[pl.ds(TOK, PART)])
    vcp = L.copy(R.va, R.vy, L.yp)
    vcp.wait_recv()
    R.vb[...] = R.va[...] + R.vy[...]
    vzc = [L.copy(R.vb, R.vz3.at[k], L.zdev[k]) for k in range(ZS - 1)]
    tick(TICKS[2][0])
    for c in vzc:
        c.wait_recv()
    R.vc[...] = R.vb[...] + R.vz3[0] + R.vz3[1] + R.vz3[2]
    vsc = L.copy(R.vc, R.vs, (L.sib, s))
    lone_end(1, lone_in, R.gres[pl.ds(0, TOK)], R.gin)
    tick(TICKS[2][1])
    vsc.wait_recv()
    R.vd[...] = R.vc[...] + R.vs[...]
    vxc = L.copy(R.vd, R.vx, (L.xp, s))
    tick(TICKS[2][2])
    vxc.wait_recv()
    R.vsum[...] = R.vd[...] + R.vx[...]
    L.settle()
    L.settle_slow()
    for total in sums:
        total.settle()


LATER = ["g1", "G1", "u1", "U1"]
TICKS = [
    {
        5: [
            "g1", "G1", "u1", "U1", "d1", "D1",
        ],
        6: [
            "o1",
        ],
    },
    {
        0: [
            "d1", "D1",
        ],
        1: [
            "g1", "G1", "u1", "U1",
        ],
        5: [
            "g1", "G1", "u1", "U1", "d1", "D1",
        ],
        6: [
            "g1", "G1", "u1", "U1", "o1", "q1", "r1",
        ],
        7: [
            "o1", "q1", "r1",
        ],
    },
    {
        0: [
            "q1", "r1", "D0", "g0", "d0",
        ],
        1: [
            "u0", "G0", "D0", "g0", "d0", "g1", "G1", "o1",
        ],
        2: [
            "u1", "U1", "q1", "r1", "q0", "U0", "u0", "G0", "D0", "g0", "d0", "o0", "r0", "q0", "U0", "u0", "G0", "D0",
            "g0", "d0", "o0", "r0", "q0", "U0", "u0", "G0", "D0", "g0", "d0", "o0", "r0", "q0", "U0", "u0", "G0", "D0",
            "g0", "d0", "o0", "r0", "q0", "U0", "u0", "G0", "D0", "g0", "d0", "o0", "r0", "q0", "U0", "u0", "G0", "D0",
            "g0", "d0", "o0", "r0", "q0", "U0", "u0", "G0", "D0", "g0", "d0", "o0", "r0", "q0", "U0", "u0", "G0", "D0",
            "g0", "d0", "o0", "r0", "q0", "U0", "u0", "G0", "D0", "g0", "d0", "o0", "r0", "q0", "U0", "u0", "G0", "o0",
            "r0", "q0", "U0", "o0", "r0", "d1", "D1", "g1", "G1", "u1", "U1", "o1", "q1", "r1",
        ],
    },
]


def rotary():
    half = HEAD // 2
    freqs = 1000.0 ** (-(np.arange(half) * 2.0 / HEAD))
    angles = np.arange(LEN)[:, None] * freqs[None, :]
    co, si = np.cos(angles), np.sin(angles)
    table = np.concatenate([co] * 4, axis=1), np.concatenate([-si, si, -si, si], axis=1)
    return [jnp.asarray(t, F32) for t in table]


def shared_device(inputs, cotangent, live, *weights):
    sets = (weights[:9], weights[9:])
    d = lax.axis_index("dp")
    cosf, sinf = rotary()
    norms = jnp.concatenate([jnp.pad(sets[i][j].astype(F32), (0, 64)) for i in range(2) for j in (2, 3, 7, 8)]).reshape(8, 256)
    flags = jnp.broadcast_to(live.astype(F32), (2, 256))
    aux = jnp.concatenate([norms, flags, jnp.zeros((6, 256), F32)], axis=0)
    args = [inputs[:, 0], cotangent[:, 0], aux]
    for i in range(2):
        args += [sets[i][0], sets[i][4], sets[i][5], sets[i][1], sets[i][6]]
    args += [cosf, sinf]
    outs = OUTS + OUTS_ANY
    res = pl.pallas_call(
        whole_kernel,
        name="layers",
        out_shape=[jax.ShapeDtypeStruct(*o) for _, o in outs],
        in_specs=[pl.BlockSpec(memory_space=pl.ANY if n in INS_ANY else pltpu.VMEM) for n in INS],
        out_specs=[pl.BlockSpec(memory_space=pltpu.VMEM)] * len(OUTS) + [pl.BlockSpec(memory_space=pl.ANY)] * len(OUTS_ANY),
        scratch_shapes=[pltpu.VMEM(*o) for _, o in SCRATCH]
        + [
            pltpu.SemaphoreType.DMA((SEMS,)),
            pltpu.SemaphoreType.DMA((SEMS,)),
            pltpu.SemaphoreType.DMA((64,)),
        ],
        cost_estimate=pl.CostEstimate(flops=4 * 10**10, bytes_accessed=5 * 10**7, transcendentals=10**7),
        compiler_params=pltpu.CompilerParams(collective_id=1, has_side_effects=True, vmem_limit_bytes=VMEM_LIMIT),
    )(*args)
    grads = pl.pallas_call(
        widen_kernel,
        name="widen",
        out_shape=[jax.ShapeDtypeStruct(*o) for o in GRADS + GRADS + [((2, TOK, D), BF16)] * 2],
        in_specs=[pl.BlockSpec(memory_space=pl.ANY)] * 4,
        out_specs=[pl.BlockSpec(memory_space=pl.ANY)] * 12,
        scratch_shapes=[
            pltpu.VMEM((2, BLOCKS, QR, D), BF16),
            pltpu.VMEM((STAGES, QR, D), F32),
            pltpu.SemaphoreType.DMA((12,)),
            pltpu.SemaphoreType.DMA((STAGES,)),
        ],
        cost_estimate=pl.CostEstimate(flops=10**7, bytes_accessed=3 * 10**7, transcendentals=0),
        compiler_params=pltpu.CompilerParams(vmem_limit_bytes=40 * 2**20),
    )(res[3], res[4], res[0], res[1])
    vsum = lax.dynamic_slice_in_dim(res[2], d * QR, QR, 1)
    out = [grads[10][:, None], grads[11][:, None]]
    for i in range(2):
        g_qkv, g_out, g_gate, g_up, g_down = grads[5 * i : 5 * i + 5]
        v = vsum[4 * i : 4 * i + 4]
        out += [g_qkv, g_out, v[0], v[1], g_gate, g_up, g_down, v[2], v[3]]
    return tuple(out)


def fits(mesh):
    return mesh.shape["dp"] == DP and mesh.shape["seq"] == SQ


def as_sent(array):
    return jax.tree.map(lambda a: a.astype(jnp.bfloat16) if a.dtype == jnp.float32 else a, array)


def tables(positions):
    half = HEAD // 2
    freqs = 1000.0 ** (-(jnp.arange(half).astype(jnp.float32) * 2.0 / HEAD))
    angles = positions[:, None] * freqs[None, :]
    return (jnp.cos(angles), jnp.sin(angles))


def rotate(values, cosine, sine):
    half = HEAD // 2
    first = values[..., :half]
    second = values[..., half:]
    cos_b = cosine[:, None, :]
    sin_b = sine[:, None, :]
    return jnp.concatenate(
        [first * cos_b - second * sin_b, second * cos_b + first * sin_b], axis=-1
    )


def unrotate(values, cosine, sine):
    half = HEAD // 2
    first = values[..., :half]
    second = values[..., half:]
    cos_b = cosine[:, None, :]
    sin_b = sine[:, None, :]
    return jnp.concatenate(
        [first * cos_b + second * sin_b, second * cos_b - first * sin_b], axis=-1
    )


def layer_norm(rows, gain, shift):
    center = rows - jnp.mean(rows, axis=-1, keepdims=True)
    spread = jnp.mean(center * center, axis=-1, keepdims=True)
    return center * lax.rsqrt(spread + 1e-05) * gain + shift


def dot_first(left, right):
    return lax.dot_general(
        left, right, (((0,), (0,)), ((), ())), preferred_element_type=jnp.float32
    )


def dot_last(left, right):
    return lax.dot_general(
        left, right, (((1,), (1,)), ((), ())), preferred_element_type=jnp.float32
    )


def forward_layer(hidden_in, weights, cosine, sine):
    w_qkv, w_out, gain_a, shift_a, w_gate, w_up, w_down, gain_f, shift_f = weights
    tokens = hidden_in.shape[0]
    width = hidden_in.shape[1]
    heads = width // HEAD
    scale = HEAD ** (-0.5)
    act = hidden_in.astype(jnp.bfloat16)
    joint = jnp.dot(act, w_qkv, preferred_element_type=jnp.float32)
    query = joint[:, :width].reshape(tokens, heads, HEAD)
    keys = joint[:, width : 2 * width].reshape(tokens, heads, HEAD)
    query_r = rotate(query, cosine, sine).astype(jnp.bfloat16)
    keys_r = rotate(keys, cosine, sine).astype(jnp.bfloat16).reshape(tokens, width)
    values_r = joint[:, 2 * width :].astype(jnp.bfloat16)
    keys_all, values_all = (
        lax.all_gather(keys_r, "seq", axis=0, tiled=True),
        lax.all_gather(values_r, "seq", axis=0, tiled=True),
    )
    length = keys_all.shape[0]
    keys_all = keys_all.reshape(length, heads, HEAD)
    values_all = values_all.reshape(length, heads, HEAD)
    scores = (
        jnp.einsum("qhd,khd->hqk", query_r, keys_all, preferred_element_type=jnp.float32) * scale
    )
    top = jnp.max(scores, axis=-1, keepdims=True)
    expo = jnp.exp(scores - top)
    total = jnp.sum(expo, axis=-1, keepdims=True)
    probs = expo / total
    log_total = top + jnp.log(total)
    context = jnp.einsum(
        "hqk,khd->qhd", probs.astype(jnp.bfloat16), values_all, preferred_element_type=jnp.float32
    )
    context = context.reshape(tokens, width).astype(jnp.bfloat16)
    res_a = hidden_in + jnp.dot(context, w_out, preferred_element_type=jnp.float32)
    norm_a = layer_norm(res_a, gain_a.astype(jnp.float32), shift_a.astype(jnp.float32))
    act_f = norm_a.astype(jnp.bfloat16)
    gate_pre = jnp.dot(act_f, w_gate, preferred_element_type=jnp.float32)
    up_pre = jnp.dot(act_f, w_up, preferred_element_type=jnp.float32)
    hidden = (jax.nn.silu(gate_pre) * up_pre).astype(jnp.bfloat16)
    res_f = norm_a + jnp.dot(hidden, w_down, preferred_element_type=jnp.float32)
    result = layer_norm(res_f, gain_f.astype(jnp.float32), shift_f.astype(jnp.float32))
    saved = (
        act,
        query_r,
        keys_r,
        values_r,
        log_total,
        context,
        res_a,
        act_f,
        gate_pre,
        up_pre,
        hidden,
        res_f,
    )
    return (result, saved)


def backward_layer(grad_out, weights, saved, cosine, sine):
    w_qkv, w_out, gain_a, shift_a, w_gate, w_up, w_down, gain_f, shift_f = weights
    (
        act,
        query_r,
        keys_r,
        values_r,
        log_total,
        context,
        res_a,
        act_f,
        gate_pre,
        up_pre,
        hidden,
        res_f,
    ) = saved
    tokens = act.shape[0]
    width = act.shape[1]
    heads = width // HEAD
    scale = HEAD ** (-0.5)
    unused, pull_f = jax.vjp(
        layer_norm, res_f, gain_f.astype(jnp.float32), shift_f.astype(jnp.float32)
    )
    d_res_f, d_gain_f, d_shift_f = pull_f(grad_out)
    d_branch = d_res_f.astype(jnp.bfloat16)
    g_down = dot_first(hidden, d_branch)
    d_hidden = dot_last(d_branch, w_down)
    sigm = jax.nn.sigmoid(gate_pre)
    d_gate = (d_hidden * up_pre * sigm * (1.0 + gate_pre * (1.0 - sigm))).astype(jnp.bfloat16)
    d_up = (d_hidden * gate_pre * sigm).astype(jnp.bfloat16)
    g_gate = dot_first(act_f, d_gate)
    g_up = dot_first(act_f, d_up)
    d_norm_a = d_res_f + dot_last(d_gate, w_gate) + dot_last(d_up, w_up)
    unused, pull_a = jax.vjp(
        layer_norm, res_a, gain_a.astype(jnp.float32), shift_a.astype(jnp.float32)
    )
    d_res_a, d_gain_a, d_shift_a = pull_a(d_norm_a)
    d_attn = d_res_a.astype(jnp.bfloat16)
    g_out = dot_first(context, d_attn)
    d_context = dot_last(d_attn, w_out).astype(jnp.bfloat16).reshape(tokens, heads, HEAD)
    keys_all, values_all = (
        lax.all_gather(keys_r, "seq", axis=0, tiled=True),
        lax.all_gather(values_r, "seq", axis=0, tiled=True),
    )
    length = keys_all.shape[0]
    keys_all = keys_all.reshape(length, heads, HEAD)
    values_all = values_all.reshape(length, heads, HEAD)
    scores = (
        jnp.einsum("qhd,khd->hqk", query_r, keys_all, preferred_element_type=jnp.float32) * scale
    )
    probs = jnp.exp(scores - log_total)
    d_probs = jnp.einsum("qhd,khd->hqk", d_context, values_all, preferred_element_type=jnp.float32)
    inner = jnp.sum(probs * d_probs, axis=-1, keepdims=True)
    d_scores = (probs * (d_probs - inner)).astype(jnp.bfloat16)
    d_query = (
        jnp.einsum("hqk,khd->qhd", d_scores, keys_all, preferred_element_type=jnp.float32) * scale
    )
    d_keys_all = (
        jnp.einsum("hqk,qhd->khd", d_scores, query_r, preferred_element_type=jnp.float32) * scale
    )
    d_values_all = jnp.einsum(
        "hqk,qhd->khd", probs.astype(jnp.bfloat16), d_context, preferred_element_type=jnp.float32
    )
    d_keys, d_values = (
        lax.psum_scatter(
            d_keys_all.reshape(length, width).astype(jnp.bfloat16),
            "seq",
            scatter_dimension=0,
            tiled=True,
        ).astype(jnp.float32),
        lax.psum_scatter(
            d_values_all.reshape(length, width).astype(jnp.bfloat16),
            "seq",
            scatter_dimension=0,
            tiled=True,
        ).astype(jnp.float32),
    )
    d_query = unrotate(d_query, cosine, sine).reshape(tokens, width)
    d_keys = unrotate(d_keys.reshape(tokens, heads, HEAD), cosine, sine).reshape(tokens, width)
    d_joint = jnp.concatenate([d_query, d_keys, d_values], axis=1).astype(jnp.bfloat16)
    g_qkv = dot_first(act, d_joint)
    grad_in = d_res_a + dot_last(d_joint, w_qkv)
    return (grad_in, (g_qkv, g_out, d_gain_a, d_shift_a, g_gate, g_up, g_down, d_gain_f, d_shift_f))


def per_device(
    inputs,
    cotangent,
    live,
    first_qkv,
    first_out,
    first_gain_a,
    first_shift_a,
    first_gate,
    first_up,
    first_down,
    first_gain_f,
    first_shift_f,
    second_qkv,
    second_out,
    second_gain_a,
    second_shift_a,
    second_gate,
    second_up,
    second_down,
    second_gain_f,
    second_shift_f,
):
    local_sets = (
        (
            first_qkv,
            first_out,
            first_gain_a,
            first_shift_a,
            first_gate,
            first_up,
            first_down,
            first_gain_f,
            first_shift_f,
        ),
        (
            second_qkv,
            second_out,
            second_gain_a,
            second_shift_a,
            second_gate,
            second_up,
            second_down,
            second_gain_f,
            second_shift_f,
        ),
    )
    micro = inputs.shape[0]
    tokens = inputs.shape[2]
    groups = lax.axis_size("dp")
    positions = (lax.axis_index("seq") * tokens + jnp.arange(tokens)).astype(jnp.float32)
    cosine, sine = tables(positions)
    totals = [
        tuple(
            (jnp.zeros((w.shape[0] * groups,) + w.shape[1:], jnp.float32) for w in local_sets[0])
        ),
        tuple(
            (jnp.zeros((w.shape[0] * groups,) + w.shape[1:], jnp.float32) for w in local_sets[1])
        ),
    ]
    results = []
    grads_in = []
    for batch in range(micro):
        flag = live[batch, 0].astype(jnp.float32)
        state = inputs[batch, 0].astype(jnp.float32)
        held = []
        saves = []
        for index in range(2):
            full = lax.all_gather(as_sent(local_sets[index]), "dp", axis=0, tiled=True)
            held.append(full)
            state, saved = forward_layer(state, full, cosine, sine)
            saves.append(saved)
        results.append((state * flag).astype(jnp.bfloat16))
        grad = cotangent[batch, 0].astype(jnp.float32) * flag
        for index in (1, 0):
            full = lax.all_gather(as_sent(local_sets[index]), "dp", axis=0, tiled=True)
            grad, terms = backward_layer(grad, full, saves[index], cosine, sine)
            totals[index] = tuple((old + new for old, new in zip(totals[index], terms)))
        grads_in.append(grad.astype(jnp.bfloat16))
    summed = []
    for index in range(2):
        shares = jax.tree.map(
            lambda part: part.astype(jnp.float32),
            lax.psum_scatter(as_sent(totals[index]), "dp", scatter_dimension=0, tiled=True),
        )
        final = jax.tree.map(
            lambda part: part.astype(jnp.float32), lax.psum(as_sent(shares), "seq")
        )
        summed.extend(final)
    output = jnp.stack(results)[:, None]
    input_grad = jnp.stack(grads_in)[:, None]
    return (output, input_grad) + tuple(summed)


def solution(mesh):
    def device(inputs, cotangent, *rest):
        if fits(mesh) and inputs.shape == (2, 1, TOK, D):
            return shared_device(inputs, cotangent, *rest)
        return per_device(inputs, cotangent, *rest)

    return jax.shard_map(
        device,
        mesh=mesh,
        in_specs=(
            P(None, "dp", "seq", None),
            P(None, "dp", "seq", None),
            P(None, "dp"),
            P("dp", None),
            P("dp", None),
            P("dp"),
            P("dp"),
            P("dp", None),
            P("dp", None),
            P("dp", None),
            P("dp"),
            P("dp"),
            P("dp", None),
            P("dp", None),
            P("dp"),
            P("dp"),
            P("dp", None),
            P("dp", None),
            P("dp", None),
            P("dp"),
            P("dp"),
        ),
        out_specs=(
            P(None, "dp", "seq", None),
            P(None, "dp", "seq", None),
            P("dp", None),
            P("dp", None),
            P("dp"),
            P("dp"),
            P("dp", None),
            P("dp", None),
            P("dp", None),
            P("dp"),
            P("dp"),
            P("dp", None),
            P("dp", None),
            P("dp"),
            P("dp"),
            P("dp", None),
            P("dp", None),
            P("dp", None),
            P("dp"),
            P("dp"),
        ),
        check_vma=False,
    )
```

```python
import functools

import jax
import jax.numpy as jnp
import numpy as np
from jax import lax
from jax.experimental import pallas as pl
from jax.experimental.pallas import tpu as pltpu
from jax.sharding import PartitionSpec as P

HEAD = 64

DP = 4
SQ = 8
TOK = 128
PART = TOK // DP
ROWS = TOK + PART
ALL = DP * ROWS
HALF = 2 * ROWS
D = 768
LEN = SQ * TOK
QB = 256
F32 = jnp.float32
BF16 = jnp.bfloat16
VMEM_LIMIT = 64 * 2**20
MESH = pl.DeviceIdType.MESH


def mm(a, b):
    return lax.dot_general(a, b, (((1,), (0,)), ((), ())), preferred_element_type=F32)


def mm_t(a, b):
    return lax.dot_general(a, b, (((1,), (1,)), ((), ())), preferred_element_type=F32)


def t_mm(a, b):
    return lax.dot_general(a, b, (((0,), (0,)), ((), ())), preferred_element_type=F32)


def low_lanes(shape):
    return lax.rem(lax.broadcasted_iota(jnp.int32, shape, len(shape) - 1), 128) < 64


def swap_halves(x):
    lane = lax.broadcasted_iota(jnp.int32, x.shape, 1)
    return jnp.where(lax.rem(lane, 64) < 32, pltpu.roll(x, 96, 1), pltpu.roll(x, 32, 1))


def flip(x):
    return pltpu.roll(x, 64, 1)


class Links:
    def __init__(self, send, recv, lsem):
        self.send, self.recv, self.used, self.sent, self.slow = send, recv, 0, [], []
        self.lsem, self.locals_used = lsem, 0
        self.d = lax.axis_index("dp")
        self.s = lax.axis_index("seq")
        self.x = self.d // 2
        self.core = lax.rem(self.d, 2)
        self.sib = 2 * self.x + (1 - self.core)
        self.xp = lax.rem(self.d + 2, DP)
        self.diag = lax.rem(self.sib + 2, DP)
        self.z = self.s // 2
        self.y = lax.rem(self.s, 2)
        self.dp_peers = [self.xp, self.diag, self.sib]
        self.seq_peers = [lax.rem(self.s + k, SQ) for k in range(1, SQ)]
        self.yp = (self.d, 2 * self.z + (1 - self.y))
        self.zp = [lax.rem(self.z + k, ZS) for k in range(1, ZS)]
        self.zdev = [(self.d, 2 * p + self.y) for p in self.zp]

    def enter(self):
        peers = [(p, self.s) for p in self.dp_peers] + [(self.d, p) for p in self.seq_peers]
        bar = pltpu.get_barrier_semaphore()
        for p in peers:
            pl.semaphore_signal(bar, inc=1, device_id=p, device_id_type=MESH)
        pl.semaphore_wait(bar, len(peers))

    def describe(self, i, src, dst, to, j=None):
        return pltpu.make_async_remote_copy(
            src_ref=src,
            dst_ref=dst,
            send_sem=self.send.at[i],
            recv_sem=self.recv.at[i if j is None else j],
            device_id=to,
            device_id_type=MESH,
        )

    def local(self, src, dst):
        c = pltpu.make_async_copy(src, dst, self.lsem.at[self.locals_used])
        self.locals_used += 1
        c.start()
        return c

    def copy(self, src, dst, to, slow=False):
        c = self.describe(self.used, src, dst, to)
        self.used += 1
        c.start()
        (self.slow if slow else self.sent).append(c)
        return c

    def settle(self):
        for c in self.sent:
            c.wait_send()
        self.sent = []

    def settle_slow(self):
        for c in self.slow:
            c.wait_send()
        self.slow = []


def span(i, rows):
    return pl.ds(pl.multiple_of(i * rows, 16), rows)


def normalize(res):
    cen = res - jnp.mean(res, axis=-1, keepdims=True)
    rstd = lax.rsqrt(jnp.mean(cen * cen, axis=-1, keepdims=True) + 1e-05)
    return cen * rstd, rstd


def normalize_back(grad, gain, xhat, rstd):
    dn = grad * gain
    return (dn - jnp.mean(dn, axis=-1, keepdims=True) - xhat * jnp.mean(dn * xhat, axis=-1, keepdims=True)) * rstd


def pack_pairs(src, dst):
    half = dst.shape[-1]
    one, two = pl.ds(0, half), pl.ds(half, half)
    keep = low_lanes((TOK, half))
    for e in range(DP):
        dst[e] = src[pl.ds(ROWS * e, TOK), one]
        dst[4, pl.ds(PART * e, PART)] = src[pl.ds(ROWS * e + TOK, PART), one]
        dst[7, pl.ds(PART * e, PART)] = src[pl.ds(ROWS * e + TOK, PART), two]
    for p in range(2):
        a = src[pl.ds(ROWS * 2 * p, TOK), two].astype(F32)
        b = src[pl.ds(ROWS * (2 * p + 1), TOK), two].astype(F32)
        dst[5 + p] = jnp.where(keep, a, b).astype(BF16)


def unpack_pairs(src, dst):
    half = src.shape[-1]
    one, two = pl.ds(0, half), pl.ds(half, half)
    keep = low_lanes((TOK, half))
    third = [src[5].astype(F32), src[6].astype(F32)]
    last = jnp.where(keep, src[7].astype(F32), 0.0).astype(BF16)
    for e in range(DP):
        dst[pl.ds(ROWS * e, TOK), one] = src[e]
        mine = third[e // 2]
        mine = jnp.where(keep, mine, 0.0) if e % 2 == 0 else jnp.where(keep, 0.0, mine)
        dst[pl.ds(ROWS * e, TOK), two] = mine.astype(BF16)
        dst[pl.ds(ROWS * e + TOK, PART), one] = src[4, pl.ds(PART * e, PART)]
        dst[pl.ds(ROWS * e + TOK, PART), two] = last[PART * e : PART * (e + 1)]


class Sums:
    def __init__(self, L, plan, g, ab, f, bufs):
        self.L, self.plan, self.g, self.ab, self.f, self.bufs = L, plan, g, ab, f, bufs
        self.end = L.z // 2
        self.outer = lax.rem(L.z, ZS - 1) == 0
        self.inner = lax.rem(L.z, ZS - 1) != 0
        self.inward = (L.d, 2 * (1 + self.end) + L.y)
        self.outward = (L.d, 2 * (3 * self.end) + L.y)
        self.across = (L.d, 2 * (3 - L.z) + L.y)
        self.outer_sent, self.inner_sent, self.todo = [], [], {}

    def send(self, role, i, j, src, dst, to):
        def make():
            return self.L.describe(i, src(), dst(), to, j)

        make().start()
        role.append(make)

    def send_all(self, i, src, dst, to):
        c = self.L.describe(i, src, dst, to)
        c.start()
        self.L.slow.append(c)

    def got(self, i, ref):
        self.L.describe(i, ref, ref, self.L.yp).wait_recv()

    def start(self, name):
        kind = self.plan[name][4]
        self.todo[name] = (self.direct_steps if kind == "d" else self.chain_steps)(name)
        next(self.todo[name])

    def advance(self, name):
        next(self.todo[name], None)

    def add(self, where, more):
        self.g[where] = (self.g[where].astype(F32) + more[...].astype(F32)).astype(BF16)

    def prepare(self, name):
        at, n, off, width, kind, k0 = self.plan[name][:6]
        i, l = self.L.used, self.L.locals_used
        self.L.used += 11
        self.L.locals_used += 1
        rows = lambda e: pl.ds(pl.multiple_of(e * HR, HR), HR)
        cols = lambda e: pl.ds(pl.multiple_of(e * YC + off, 128), width)
        return i, l, at, pl.ds(at, n), pl.ds(k0, n), rows, cols

    def chain_steps(self, name):
        L, g, f = self.L, self.g, self.f
        i, l, at, r, b, rows, cols = self.prepare(name)
        end, y = self.end, L.y
        k0 = self.plan[name][5]
        zfirst = self.plan[name][4] == "z"
        off, width = self.plan[name][2:4]
        within = pl.ds(off, width)
        half = self.bufs.rh.at[b, :, within] if zfirst else None
        ab = self.ab
        if zfirst:
            piece = lambda e: (r, slice(None), cols(e))
            first, second = self.bufs.zf.at[b, :, within], self.bufs.zs.at[b, :, within]
            spare = self.bufs.zf
            final = (r, rows(y), cols(end))
        else:
            piece = lambda e: (r, rows(e), cols(y))
            first, second = self.bufs.pf.at[b, :, within], self.bufs.ps.at[b, :, within]
            spare = self.bufs.pf
            ry = self.bufs.ry.at[b, :, within]
            final = (r, rows(end), cols(y))

        def across_dp(k):
            p = L.dp_peers[k]
            return L.describe(i + 3 + k, spare.at[k0 + p, pl.ds(0, HR), within], ab.at[at + L.d, :, within], (p, L.s))

        local = lambda: pltpu.make_async_copy(ab.at[r, :, within], f.at[final], L.lsem.at[l])

        if not zfirst:
            self.send_all(i, g.at[r, :, cols(1 - y)], ry, L.yp)
            yield
            self.got(i, ry)
            self.add((r, slice(None), cols(y)), ry)

        @pl.when(self.outer)
        def _():
            self.send(self.outer_sent, i + 1, i + 1, lambda: g.at[piece(1 - end)], lambda: first, self.inward)

        yield

        @pl.when(self.inner)
        def _():
            self.got(i + 1, first)
            self.add(piece(1 - end), first)
            self.send(self.inner_sent, i + 1, i + 2, lambda: g.at[piece(1 - end)], lambda: second, self.across)

        yield

        @pl.when(self.inner)
        def _():
            self.got(i + 2, second)
            self.add(piece(end), second)
            self.send(self.inner_sent, i + 2, i + 2, lambda: g.at[piece(end)], lambda: second, self.outward)

        yield
        if zfirst:

            @pl.when(self.outer)
            def _():
                self.got(i + 2, second)
                self.add(piece(end), second)
                self.send(self.outer_sent, i, i, lambda: g.at[r, rows(1 - y), cols(end)], lambda: half, L.yp)

            yield

        @pl.when(self.outer)
        def _():
            if zfirst:
                self.got(i, half)
                total = g[final].astype(F32) + half[...].astype(F32)
            else:
                self.got(i + 2, second)
                total = g[final].astype(F32) + second[...].astype(F32)
            if at < 12:
                spare[b, pl.ds(0, HR), within] = total.astype(BF16)
                for k in range(DP - 1):
                    across_dp(k).start()
                ab[at + L.d, :, within] = spare[k0 + L.d, pl.ds(0, HR), within]
            else:
                ab[r, :, within] = total.astype(BF16)

        yield

        @pl.when(self.outer)
        def _():
            if at < 12:
                for k in range(DP - 1):
                    across_dp(k).wait()
            self.send(self.outer_sent, i + 6, i + 6, lambda: ab.at[r, :, within], lambda: f.at[final], L.yp if zfirst else self.inward)
            local().start()

        yield
        if zfirst:

            @pl.when(self.outer)
            def _():
                self.got(i + 6, ab.at[r, :, within])
                local().wait()
                self.send(self.outer_sent, i + 9, i + 9, lambda: f.at[piece(end)], lambda: f.at[piece(end)], self.inward)

            yield

        @pl.when(self.inner)
        def _():
            self.got(i + (9 if zfirst else 6), f.at[piece(end)])
            self.send(self.inner_sent, i + 7, i + 7, lambda: f.at[piece(end)], lambda: f.at[piece(end)], self.across)

        yield

        @pl.when(self.inner)
        def _():
            self.got(i + 7, f.at[piece(1 - end)])
            self.send(self.inner_sent, i + 8, i + 8, lambda: f.at[piece(1 - end)], lambda: f.at[piece(1 - end)], self.outward)

        yield

        @pl.when(self.outer)
        def _():
            self.got(i + 8, f.at[piece(1 - end)])
            if not zfirst:
                local().wait()

        if not zfirst:
            whole = f.at[r, :, cols(y)]
            self.send_all(i + 9, whole, whole, L.yp)
            yield
            self.got(i + 9, whole)

    def direct_steps(self, name):
        L, g, f = self.L, self.g, self.f
        i, l, at, r, b, rows, cols = self.prepare(name)
        n, off, width = self.plan[name][1:4]
        mine = cols(L.y)
        within = pl.ds(off, width)
        ry = self.bufs.ry.at[b, :, within]
        quarter = lambda z: pl.ds(pl.multiple_of(z * (HR // 2), HR // 2), HR // 2)
        own = (r, quarter(L.z), mine)
        k1 = self.plan[name][6]
        c = pl.ds(k1, n)
        got, out, ab = self.bufs.qz, self.bufs.qo, self.bufs.qa
        self.send_all(i, g.at[r, :, cols(1 - L.y)], ry, L.yp)
        yield
        self.got(i, ry)
        self.add((r, slice(None), mine), ry)
        for k in range(ZS - 1):
            self.send_all(i + 1 + k, g.at[r, quarter(L.zp[k]), mine], got.at[k, c, :, within], L.zdev[k])
        yield
        total = g[own].astype(F32)
        for k in range(ZS - 1):
            self.got(i + 1 + k, got.at[k, c, :, within])
            total = total + got[k, c, :, within].astype(F32)
        if at < 12:
            out[c, :, within] = total.astype(BF16)
            for k, p in enumerate(L.dp_peers):
                self.send_all(i + 4 + k, out.at[k1 + p, :, within], ab.at[k1 + L.d, :, within], (p, L.s))
            ab[k1 + L.d, :, within] = out[k1 + L.d, :, within]
            yield
            for k in range(DP - 1):
                self.got(i + 4 + k, ab.at[k1, :, within])
        else:
            ab[c, :, within] = total.astype(BF16)
        local = pltpu.make_async_copy(ab.at[c, :, within], f.at[own], L.lsem.at[l])
        local.start()
        for k in range(ZS - 1):
            self.send_all(i + 7 + k, ab.at[c, :, within], f.at[own], L.zdev[k])
        yield
        local.wait()
        for k in range(ZS - 1):
            self.got(i + 7 + k, f.at[own])
        whole = f.at[r, :, mine]
        self.send_all(i + 10, whole, whole, L.yp)
        yield
        self.got(i + 10, whole)

    def settle(self):
        @pl.when(self.outer)
        def _():
            for make in self.outer_sent:
                make().wait_send()

        @pl.when(self.inner)
        def _():
            for make in self.inner_sent:
                make().wait_send()


class Stage:
    def __init__(self, buf, sem):
        self.buf, self.sem, self.count, self.open = buf, sem, 0, {}

    def slot(self):
        i = self.count % STAGES
        if i in self.open:
            self.open.pop(i).wait()
        return self.buf.at[i]

    def go(self, dst):
        i = self.count % STAGES
        c = pltpu.make_async_copy(self.buf.at[i], dst, self.sem.at[i])
        c.start()
        self.open[i] = c
        self.count += 1

    def settle(self):
        for c in self.open.values():
            c.wait()


def widen_kernel(f0, f1, rows_out, rows_in, *refs):
    outs, (o_out, o_in, buf, stage_buf, in_sem, out_sem) = refs[:10], refs[10:]
    stage = Stage(stage_buf, out_sem)
    moves = [
        pltpu.make_async_copy(rows_out, o_out, in_sem.at[10]),
        pltpu.make_async_copy(rows_in, o_in, in_sem.at[11]),
    ]
    for c in moves:
        c.start()
    keep = low_lanes((QR, 128))
    loads = {}
    for l, f in ((0, f0), (1, f1)):
        for k, (at, n) in enumerate(CHUNKS.values()):
            c = pltpu.make_async_copy(f.at[pl.ds(at, n)], buf.at[l, pl.ds(at, n)], in_sem.at[5 * l + k])
            c.start()
            loads[5 * l + k] = c
    for l in range(2):
        o_qkv, o_out, o_gate, o_up, o_down = outs[5 * l : 5 * l + 5]
        g = buf.at[l]
        for k, (name, (at, n)) in enumerate(CHUNKS.items()):
            loads[5 * l + k].wait()
            for i in range(3 if name == "qkv" else n):
                st = stage.slot()
                if name == "qkv":
                    one, two = pl.ds(128 * i, 128), pl.ds(384 + 128 * i, 128)
                    for a in range(2):
                        po = flip(g[2 * a + 1, :, one].astype(F32))
                        te, to = g[2 * a, :, two].astype(F32), g[2 * a + 1, :, two].astype(F32)
                        st[:, pl.ds(384 * a, 128)] = g[2 * a, :, one].astype(F32)
                        st[:, pl.ds(384 * a + 128, 128)] = jnp.where(keep, te + flip(te), po)
                        st[:, pl.ds(384 * a + 256, 128)] = jnp.where(keep, po, to + flip(to))
                    dst = o_qkv.at[:, pl.ds(D * i, D)]
                else:
                    st[...] = g[at + i].astype(F32)
                    if name == "out":
                        dst = o_out
                    elif name == "down":
                        dst = o_down.at[pl.ds(QR * i, QR)]
                    else:
                        dst = (o_gate if name == "gate" else o_up).at[:, pl.ds(D * i, D)]
                stage.go(dst)
    stage.settle()
    for c in moves:
        c.wait()


CHUNKS = {"qkv": (0, 4), "gate": (4, 4), "up": (8, 4), "down": (12, 4), "out": (16, 1)}
BLOCKS = 17
ZS = 4
QR = D // DP
HR = QR // 2
YC = D // 2
PLAN = [
    {
        "d": (12, 4, 0, 256, "y", 0, 0),
        "D": (12, 4, 256, 128, "y", 0, 0),
        "g": (4, 4, 0, 256, "z", 0, 0),
        "G": (4, 4, 256, 128, "z", 0, 0),
        "u": (8, 4, 0, 256, "y", 4, 0),
        "U": (8, 4, 256, 128, "y", 4, 0),
        "o": (16, 1, 0, YC, "y", 8, 0),
        "q": (0, 4, 0, 256, "d", 9, 0),
        "r": (0, 4, 256, 128, "d", 9, 0),
    },
    {
        "d": (12, 4, 0, 256, "d", 12, 12),
        "D": (12, 4, 256, 128, "d", 12, 12),
        "g": (4, 4, 0, 256, "d", 4, 4),
        "G": (4, 4, 256, 128, "d", 4, 4),
        "u": (8, 4, 0, 256, "d", 8, 8),
        "U": (8, 4, 256, 128, "d", 8, 8),
        "o": (16, 1, 0, YC, "d", 16, 16),
        "q": (0, 4, 0, 256, "d", 0, 0),
        "r": (0, 4, 256, 128, "d", 0, 0),
    },
]
STAGES = 8
SEMS = 480

INS = ["inp", "cot", "aux", "wq0", "wg0", "wu0", "wo0", "wd0", "wq1", "wg1", "wu1", "wo1", "wd1", "cosf", "sinf"]
INS_ANY = {"wq0", "wg0", "wu0", "wd0", "wq1", "wg1", "wu1", "wd1"}
GRADS = [((QR, 3 * D), F32), ((QR, D), F32), ((QR, DP * D), F32), ((QR, DP * D), F32), ((D, D), F32)]
BIG = ((ALL, D), BF16)
OUTS = [("out", ((2, TOK, D), BF16)), ("gin", ((2, TOK, D), BF16)), ("vsum", ((8, D), F32))]
OUTS_ANY = [("fs" + str(i), ((BLOCKS, QR, D), BF16)) for i in range(2)] + [("st" + str(i), BIG) for i in range(5)] + [("sx0", ((ROWS, D), F32)), ("sx1", ((ROWS, D), F32)), ("sx2", ((LEN, 128), F32))]
TALL = ((LEN, 128), BF16)
SCRATCH = (
    [
        (n + str(l), s)
        for l in range(2)
        for n, s in [
            ("qkv", ((LEN, 384), BF16)),
            ("lse", ((8, LEN), F32)),
            ("ce", ((ALL, 256), BF16)),
            ("ra", ((ROWS, 128), F32)),
            ("rf", ((ROWS, 128), F32)),
            ("wqg", ((D, D), BF16)),
            ("wgg", ((D, D), BF16)),
            ("wug", ((D, D), BF16)),
            ("wog", ((256, D), BF16)),
            ("g", ((BLOCKS, QR, D), BF16)),
            ("ry", ((13 + 4 * l, QR, YC), BF16)),
            ("qz", ((ZS - 1, 4 + 13 * l, HR // 2, YC), BF16)),
            ("qo", ((4 + 13 * l, HR // 2, YC), BF16)),
            ("qa", ((4 + 13 * l, HR // 2, YC), BF16)),
        ]
    ]
    + [
        ("x", BIG),
        ("wd", ((D, D), BF16)),
        ("xa", ((ROWS, D), F32)),
        ("xf", ((ROWS, D), F32)),
        ("ctx", ((LEN, 128), F32)),
        ("actf", BIG),
        ("gp", BIG),
        ("up", BIG),
        ("hid", BIG),
        ("part", ((ALL, D), F32)),
        ("ta", BIG),
        ("tb", BIG),
        ("db", BIG),
        ("dsb", BIG),
        ("sb", ((SQ, TOK, 384), BF16)),
        ("sc", ((SQ, TOK, 128), BF16)),
        ("rx", ((SQ, TOK, 384), BF16)),
        ("rc", ((SQ, TOK, 128), BF16)),
        ("dc", TALL),
        ("cb", TALL),
        ("kz", ((2, LEN, 128), BF16)),
        ("vz", ((2, LEN, 128), BF16)),
        ("kt", ((2, 128, LEN), BF16)),
        ("et", ((128, LEN), F32)),
        ("cz", ((2, LEN, 128), BF16)),
        ("inner", ((8, LEN), F32)),
        ("hres", ((ROWS, D), F32)),
        ("gres", ((ROWS, D), F32)),
        ("nv", ((8, D), F32)),
        ("auxs", ((DP, 16, 256), F32)),
        ("cbuf", ((DP, 2, PART, D), BF16)),
        ("loa", ((2, DP, PART, D), BF16)),
        ("los", ((2, PART, D), BF16)),
        ("ab", ((BLOCKS, HR, YC), BF16)),
        ("rh", ((4, HR, YC), BF16)),
        ("pf", ((9, HR, YC), BF16)),
        ("ps", ((9, HR, YC), BF16)),
        ("zf", ((4, QR, YC), BF16)),
        ("zs", ((4, QR, YC), BF16)),
        ("va", ((8, D), F32)),
        ("vb", ((8, D), F32)),
        ("vc", ((8, D), F32)),
        ("vd", ((8, D), F32)),
        ("vy", ((8, D), F32)),
        ("vz3", ((ZS - 1, 8, D), F32)),
        ("vs", ((8, D), F32)),
        ("vx", ((8, D), F32)),
    ]
    + [(n + k, s) for k in "af" for n, s in [("snd", ((2, ROWS, D), BF16)), ("got", ((2, ROWS, D), BF16)), ("mid", ((ROWS, D), BF16)), ("fin", ((ROWS, D), BF16))]]
)


class Named:
    pass


def whole_kernel(*refs):
    R = Named()
    names = INS + [n for n, _ in OUTS + OUTS_ANY + SCRATCH]
    for n, r in zip(names, refs):
        setattr(R, n, r)
    L = Links(*refs[len(names) :])
    d, s = L.d, L.s
    own = pl.ds(pl.multiple_of(d * ROWS, 32), ROWS)
    tok = pl.ds(pl.multiple_of(s * TOK, TOK), TOK)

    def at_layer(n, l):
        return getattr(R, n + str(l))

    def chip(c):
        return pl.ds(pl.multiple_of(c * HALF, 32), HALF)

    local = L.local

    def rows_at(ref, i):
        return ref.at[span(i, ROWS)]

    def input_at(ref, i):
        return ref.at[pl.ds(2 * i, 2), pl.ds(0, TOK)]

    def gather_begin(ref, at=rows_at):
        far = L.copy(at(ref, d), at(ref, d), (L.xp, s))
        near = L.copy(at(ref, d), at(ref, d), (L.sib, s))
        return near, far

    def gather_forward(ref, far, at=rows_at):
        far.wait_recv()
        return L.copy(at(ref, L.xp), at(ref, L.xp), (L.sib, s))

    part = R.part

    def reduce_chip(k, i):
        snd, got = getattr(R, "snd" + k), getattr(R, "got" + k)
        snd[i] = part[span(L.diag if i else L.sib, ROWS)].astype(BF16)
        return L.copy(snd.at[i], got.at[i], (L.sib, s))

    def reduce_cross(k, c_other):
        got, mid, fin = getattr(R, "got" + k), getattr(R, "mid" + k), getattr(R, "fin" + k)
        c_other.wait_recv()
        mid[...] = (part[span(L.xp, ROWS)] + got[1].astype(F32)).astype(BF16)
        return L.copy(mid, fin, (L.xp, s))

    def reduce_end(k, c_own, c_cross):
        got, fin = getattr(R, "got" + k), getattr(R, "fin" + k)
        c_own.wait_recv()
        c_cross.wait_recv()
        return part[own] + got[0].astype(F32) + fin[...].astype(F32)

    lqs = [
        [local(getattr(R, "wq" + str(l)).at[:, pl.ds(D * t, D)], R.g1.at[8 + 3 * l + t]) for t in range(3)]
        for l in range(2)
    ]
    mycols = pl.ds(pl.multiple_of(d * D, D), D)
    mydep = pl.ds(pl.multiple_of(d * QR, 64), QR)
    lws = []
    for l in range(2):
        for n in "gu":
            lws.append(local(getattr(R, "w" + n + str(l)).at[:, mycols], at_layer("w" + n + "g", l).at[mydep]))
    lws.append(local(R.wd0, R.wd))
    inb = R.g0
    inb[pl.ds(2 * d, 2), pl.ds(0, TOK)] = R.inp[...]
    R.auxs[d] = R.aux[...]
    L.enter()
    small = [L.copy(R.aux, R.auxs.at[d], (p, s)) for p in L.dp_peers]

    hq = QR // 2
    mine_half = L.y * hq

    def arrange_qkv(l):
        for c in lqs[l]:
            c.wait()
        keep = low_lanes((QR, 128))
        for t in range(3):
            for a in range(2):
                t0, t1, t2 = [R.g1[8 + 3 * l + t, :, pl.ds(384 * a + 128 * i, 128)].astype(F32) for i in range(3)]
                f1, f2 = flip(t1), flip(t2)
                for p, one, two in (
                    (2 * a, t0, jnp.where(keep, t1, f1)),
                    (2 * a + 1, jnp.where(keep, f1, f2), jnp.where(keep, f2, t2)),
                ):
                    R.g1[4 * l + p, :, pl.ds(128 * t, 128)] = one.astype(BF16)
                    R.g1[4 * l + p, :, pl.ds(384 + 128 * t, 128)] = two.astype(BF16)

    def share_qkv(l):
        w = at_layer("wqg", l)
        far = []
        for p in (L.xp, L.diag):
            src = R.g1.at[4 * l + p, pl.ds(pl.multiple_of(mine_half, 32), hq)]
            far.append(L.copy(src, w.at[pl.ds(pl.multiple_of(d * QR + mine_half, 32), hq)], (p, s), True))
        near = L.copy(R.g1.at[4 * l + L.sib], w.at[mydep], (L.sib, s), True)
        w[mydep] = R.g1[4 * l + d]
        return [(w, far, near)]

    def share_ff(l):
        res = []
        for n in "gu":
            w, g = getattr(R, "w" + n + str(l)), at_layer("w" + n + "g", l)
            far = []
            half = pl.ds(pl.multiple_of(mine_half, 32), hq)
            for p in (L.xp, L.diag):
                src = w.at[half, pl.ds(pl.multiple_of(p * D, D), D)]
                far.append(L.copy(src, g.at[pl.ds(pl.multiple_of(d * QR + mine_half, 32), hq)], (p, s), True))
            near = L.copy(w.at[:, pl.ds(pl.multiple_of(L.sib * D, D), D)], g.at[mydep], (L.sib, s), True)
            res.append((g, far, near))
        return res

    def pass_on(shares):
        res = []
        for w, far, near in shares:
            for c, p in zip(far, (L.xp, L.diag)):
                c.wait_recv()
                o = pl.ds(pl.multiple_of(p * QR + mine_half, 32), hq)
                res.append(L.copy(w.at[o], w.at[o], L.yp, True))
            res.append(near)
        return res

    arrange_qkv(0)
    sq = share_qkv(0)
    near, far = gather_begin(inb, input_at)
    for l in range(2):
        wo, wog = getattr(R, "wo" + str(l)), at_layer("wog", l)
        wog[pl.ds(0, QR)] = wo[...]
        wog[pl.ds(QR, 64)] = wo[pl.ds(128, 64)]
    arrange_qkv(1)
    for c in small:
        c.wait_recv()
    keep8 = low_lanes((8, 128))
    for a in range(2):
        e, o = R.auxs.at[2 * a], R.auxs.at[2 * a + 1]
        eight = pl.ds(0, 8)
        lo, hi = pl.ds(0, 128), pl.ds(128, 128)
        po = flip(o[eight, lo])
        R.nv[:, pl.ds(384 * a, 128)] = e[eight, lo]
        R.nv[:, pl.ds(384 * a + 128, 128)] = jnp.where(keep8, e[eight, hi], po)
        R.nv[:, pl.ds(384 * a + 256, 128)] = jnp.where(keep8, po, flip(o[eight, hi]))

    def flag(j, m):
        v = R.auxs[j, 8 + m : 9 + m]
        return jnp.concatenate([v, v, v], axis=1)

    f0 = flag(0, 0) * flag(1, 0) * flag(2, 0) * flag(3, 0)
    f1 = 1.0 - f0
    lone_flag = [f0 * flag(j, 1) + f1 * flag(j, 0) for j in range(DP)]
    lone_mine = f0 * flag(d, 1) + f1 * flag(d, 0)

    shares = pass_on(sq)
    fwd = gather_forward(inb, far, input_at)
    near.wait_recv()
    fwd.wait_recv()
    lone = None
    for j in range(DP):
        a = inb[2 * j, pl.ds(0, TOK)].astype(F32)
        b = inb[2 * j + 1, pl.ds(0, TOK)].astype(F32)
        R.x[pl.ds(ROWS * j, TOK)] = (f0 * a + f1 * b).astype(BF16)
        term = lone_flag[j] * (f0 * b + f1 * a)
        lone = term if lone is None else lone + term
    lone = lone.astype(BF16)
    for j in range(DP):
        R.x[pl.ds(ROWS * j + TOK, PART)] = lone[PART * j : PART * (j + 1)]
    R.hres[...] = R.x[own].astype(F32)
    for c in shares:
        c.wait_recv()

    later = {}
    stash = []

    def forward(l):
        x = R.x
        ctx = R.ctx
        qkv, lse, ce = [at_layer(n, l) for n in ("qkv", "lse", "ce")]
        wq, wg, wu, wo = [at_layer(n, l) for n in ("wqg", "wgg", "wug", "wog")]
        wd = R.wd
        qx = R.ta

        def project(c):
            rows = chip(c)
            a = x[rows]
            y = [mm(a, wq[:, pl.ds(256 * t, 256)]) for t in range(3)]
            for b in range(2):
                j = 2 * c + b
                lone_at = pl.ds(pl.multiple_of(s * TOK + j * PART, PART), PART)
                co = jnp.concatenate([R.cosf[tok], R.cosf[lone_at]], axis=0)
                si = jnp.concatenate([R.sinf[tok], R.sinf[lone_at]], axis=0)
                for t in range(6):
                    v = y[t // 2][ROWS * b : ROWS * (b + 1), 128 * (t % 2) : 128 * (t % 2 + 1)]
                    if t % 3 != 2:
                        v = v * co + swap_halves(v) * si
                    if t % 3 == 0:
                        v = v * (HEAD**-0.5)
                    qx[span(j, ROWS), pl.ds(128 * t, 128)] = v.astype(BF16)

        if l == 0:
            project(0)
            project(1)
            keep_x = local(x, R.st4)
        else:
            x[own] = R.hres[...].astype(BF16)
            near, far = gather_begin(x)
            near.wait_recv()
            project(L.x)
            fwd = gather_forward(x, far)
            fwd.wait_recv()
            project(1 - L.x)

        for c in stash:
            c.wait()
        del stash[:]
        pack_pairs(qx, R.sb)
        qkv[tok] = R.sb[s]
        qc = [L.copy(R.sb.at[p], qkv.at[tok], (d, p)) for p in L.seq_peers]
        cc = []
        ff = share_ff(l)
        if l == 0:
            for p in L.dp_peers:
                r = pl.ds(pl.multiple_of(p * PART, PART), PART)
                cc.append(L.copy(R.cot.at[:, r, :], R.cbuf.at[d], (p, s)))
            R.cbuf[d] = R.cot[:, pl.ds(pl.multiple_of(d * PART, PART), PART), :]
        for c in qc:
            c.wait_recv()

        keep = low_lanes((LEN, 128))
        k = qkv[:, pl.ds(128, 128)].astype(F32)
        R.kz[0] = jnp.where(keep, k, 0.0).astype(BF16)
        R.kz[1] = jnp.where(keep, 0.0, k).astype(BF16)
        base = L.used
        L.used += SQ

        def back(p, i):
            r = pl.ds(pl.multiple_of(p * TOK, TOK), TOK)
            return L.describe(i, R.cb.at[r], R.rc.at[s], (d, p))

        @pl.loop(0, LEN // QB)
        def _(i):
            at = pl.ds(pl.multiple_of(i * QB, QB), QB)
            q = qkv[at, pl.ds(0, 128)]
            outs, logs = [], []
            for j in range(2):
                sc = mm_t(q, R.kz[j])
                top = jnp.max(sc, axis=-1, keepdims=True)
                ex = jnp.exp(sc - top)
                tot = jnp.sum(ex, axis=-1, keepdims=True)
                o = mm(ex.astype(BF16), qkv[:, pl.ds(256, 128)])
                outs.append(o / tot)
                logs.append(jnp.broadcast_to(top + jnp.log(tot), (QB, 128)))
            pick = low_lanes((QB, 128))
            c = jnp.where(pick, outs[0], outs[1])
            ctx[at] = c
            R.et[:, at] = jnp.where(pick, logs[0], logs[1]).T
            R.cb[at] = c.astype(BF16)
            for h in range(QB // TOK):
                p = (QB // TOK) * i + h
                k = lax.rem(p - s + SQ, SQ)

                @pl.when(k != 0)
                def _():
                    back(p, base + k).start()

        lse[0:1] = R.et[0:1]
        lse[1:2] = R.et[64:65]
        R.rc[s] = R.cb[tok]
        ffp = pass_on(ff)
        if l == 0:
            later["q"] = share_qkv(1)
            for c in cc:
                c.wait_recv()
            a = R.cot[0].astype(F32)
            b = R.cot[1].astype(F32)
            R.gres[pl.ds(0, TOK)] = f0 * a + f1 * b
            lone = None
            for j in range(DP):
                term = lone_flag[j] * (f0 * R.cbuf[j, 1].astype(F32) + f1 * R.cbuf[j, 0].astype(F32))
                lone = term if lone is None else lone + term
            R.gres[pl.ds(TOK, PART)] = lone
        for k in range(1, SQ):
            back(L.seq_peers[k - 1], base + k).wait_recv()
        unpack_pairs(R.rc, ce)

        for c in (1 - L.x, L.x):
            a = ce[chip(c)]
            for t in range(3):
                cs = pl.ds(256 * t, 256)
                part[chip(c), cs] = mm(a, wo[:, cs])
        for k in range(1, SQ):
            back(L.seq_peers[k - 1], base + k).wait_send()
        L.settle()
        if l == 0:
            keep_x.wait()
        c_other = reduce_chip("a", 1)
        c_own = reduce_chip("a", 0)
        c_cross = reduce_cross("a", c_other)
        res = R.hres[...] + reduce_end("a", c_own, c_cross)
        n = 4 * l
        xhat, rstd = normalize(res)
        norm_a = xhat * R.nv[n : n + 1] + R.nv[n + 1 : n + 2]
        R.actf[own] = norm_a.astype(BF16)
        near, far = gather_begin(R.actf)
        R.hres[...] = norm_a
        R.xa[...] = xhat
        at_layer("ra", l)[...] = jnp.broadcast_to(rstd, (ROWS, 128))
        if l == 0:
            for c in lws:
                c.wait()
        for c in ffp:
            c.wait_recv()

        def feed(rows):
            a = R.actf[rows]
            for t in range(3):
                cs = pl.ds(256 * t, 256)
                gp = mm(a, wg[:, cs])
                up = mm(a, wu[:, cs])
                R.gp[rows, cs] = gp.astype(BF16)
                R.up[rows, cs] = up.astype(BF16)
                R.hid[rows, cs] = (gp * jax.nn.sigmoid(gp) * up).astype(BF16)
            h = R.hid[rows]
            for t in range(3):
                cs = pl.ds(256 * t, 256)
                part[rows, cs] = mm(h, wd[:, cs])

        near.wait_recv()
        feed(chip(L.x))
        L.settle()
        c_own = reduce_chip("f", 0)
        fwd = gather_forward(R.actf, far)
        fwd.wait_recv()
        feed(chip(1 - L.x))
        c_other = reduce_chip("f", 1)
        c_cross = reduce_cross("f", c_other)
        if l == 0:
            later["q"] = pass_on(later["q"])
            for i, r in enumerate((R.actf, R.gp, R.up, R.hid)):
                stash.append(local(r, getattr(R, "st" + str(i))))
            stash.append(local(R.xa, R.sx0))
            stash.append(local(R.ctx, R.sx2))
            stash.append(local(R.wd1, R.wd))
            for c in later["q"]:
                c.wait_recv()
        res = R.hres[...] + reduce_end("f", c_own, c_cross)
        xhat, rstd = normalize(res)
        h = xhat * R.nv[n + 2 : n + 3] + R.nv[n + 3 : n + 4]
        R.xf[...] = xhat
        if l == 0:
            stash.append(local(R.xf, R.sx1))
        at_layer("rf", l)[...] = jnp.broadcast_to(rstd, (ROWS, 128))
        R.hres[...] = h
        L.settle()

    def lone_begin(k, rows):
        R.los[k] = rows.astype(BF16)
        R.loa[k, d] = rows.astype(BF16)
        return [L.copy(R.los.at[k], R.loa.at[k, d], (p, s)) for p in L.dp_peers]

    def lone_end(k, copies, whole, dst):
        for c in copies:
            c.wait_recv()
        lone = lone_mine * R.loa[k].reshape(TOK, D).astype(F32)
        dst[0] = (f0 * whole + f1 * lone).astype(BF16)
        dst[1] = (f1 * whole + f0 * lone).astype(BF16)

    forward(0)
    forward(1)
    lone_out = lone_begin(0, R.hres[pl.ds(TOK, PART)])


    def tick(codes):
        for c in codes:
            total = sums[int(c[1])]
            total.advance(c[0]) if c[0] in total.todo else total.start(c[0])

    sums = []
    for l in range(2):
        bufs = Named()
        for n in ("rh", "pf", "ps", "zf", "zs"):
            setattr(bufs, n, getattr(R, n))
        for n in ("ry", "qz", "qo", "qa"):
            setattr(bufs, n, at_layer(n, l))
        sums.append(Sums(L, PLAN[l], at_layer("g", l), R.ab, at_layer("fs", l), bufs))
    R.va[...] = jnp.zeros_like(R.va)

    def backward(l, ticks):
        x = R.x
        ctx = R.ctx
        qkv, lse, ce = [at_layer(n, l) for n in ("qkv", "lse", "ce")]
        wq, wg, wu, wo = [at_layer(n, l) for n in ("wqg", "wgg", "wug", "wog")]
        wd = R.wd
        g, n, total = at_layer("g", l), 4 * l, sums[l]

        def grad_of(name, a, b):
            at, c = CHUNKS[name]
            for t in range(3):
                cs = pl.ds(256 * t, 256)
                g[pl.ds(at, c), :, cs] = t_mm(a[...], b[:, cs]).astype(BF16).reshape(c, QR, 256)
            for k in PLAN[l]:
                if PLAN[l][k][0] == at and k + str(l) not in LATER:
                    total.start(k)

        grad = R.gres[...]
        xhat = R.xf[...]
        d_res_f = normalize_back(grad, R.nv[n + 2 : n + 3], xhat, at_layer("rf", l)[:, 0:1])
        R.db[own] = d_res_f.astype(BF16)
        near, far = gather_begin(R.db)
        R.va[n + 2 : n + 3] = jnp.sum(grad * xhat, axis=0, keepdims=True)
        R.va[n + 3 : n + 4] = jnp.sum(grad, axis=0, keepdims=True)
        R.gres[...] = d_res_f
        tick(ticks.get(0, ()))

        def feed(rows):
            a = R.db[rows]
            for t in range(3):
                cs = pl.ds(256 * t, 256)
                dh = mm_t(a, wd[cs])
                gv, uv = R.gp[rows, cs].astype(F32), R.up[rows, cs].astype(F32)
                sig = jax.nn.sigmoid(gv)
                R.ta[rows, cs] = (dh * uv * sig * (1.0 + gv * (1.0 - sig))).astype(BF16)
                R.tb[rows, cs] = (dh * gv * sig).astype(BF16)
            dgv, duv = R.ta[rows], R.tb[rows]
            for t in range(3):
                cs = pl.ds(256 * t, 256)
                part[rows, cs] = mm_t(dgv, wg[cs]) + mm_t(duv, wu[cs])

        near.wait_recv()
        feed(chip(L.x))
        L.settle()
        c_own = reduce_chip("f", 0)
        fwd = gather_forward(R.db, far)
        fwd.wait_recv()
        feed(chip(1 - L.x))
        c_other = reduce_chip("f", 1)
        c_cross = reduce_cross("f", c_other)
        grad_of("down", R.hid, R.db)
        grad_of("gate", R.actf, R.ta)
        grad_of("up", R.actf, R.tb)
        tick(ticks.get(1, ()))
        d_norm = R.gres[...] + reduce_end("f", c_own, c_cross)
        L.settle()
        xhat = R.xa[...]
        d_res_a = normalize_back(d_norm, R.nv[n : n + 1], xhat, at_layer("ra", l)[:, 0:1])
        R.dsb[own] = d_res_a.astype(BF16)
        near, far = gather_begin(R.dsb)
        R.va[n : n + 1] = jnp.sum(d_norm * xhat, axis=0, keepdims=True)
        R.va[n + 1 : n + 2] = jnp.sum(d_norm, axis=0, keepdims=True)
        R.gres[...] = d_res_a
        tick(ticks.get(2, ()))
        reload = []
        if l == 1:
            for i, r in enumerate((R.actf, R.gp, R.up, R.hid)):
                reload.append(local(getattr(R, "st" + str(i)), r))
            reload.append(local(R.sx0, R.xa))
            reload.append(local(R.sx1, R.xf))
            reload.append(local(R.wd0, R.wd))
        fwd = gather_forward(R.dsb, far)
        near.wait_recv()
        fwd.wait_recv()
        R.ta[:, pl.ds(0, 256)] = mm_t(R.dsb[...], wo[...]).astype(BF16)
        pack_pairs(R.ta.at[:, pl.ds(0, 256)], R.sc)
        R.dc[tok] = R.sc[s]
        qc = [L.copy(R.sc.at[p], R.dc.at[tok], (d, p)) for p in L.seq_peers]

        g_out = t_mm(ce[...], R.dsb[...])
        o = CHUNKS["out"][0]
        g[o, pl.ds(0, 128)] = g_out[0:128].astype(BF16)
        g[o, pl.ds(128, 64)] = (g_out[128:192] + g_out[192:256]).astype(BF16)
        total.start("o")
        keep = low_lanes((LEN, 128))
        k = qkv[:, pl.ds(128, 128)].astype(F32)
        k0, k1 = jnp.where(keep, k, 0.0), jnp.where(keep, 0.0, k)
        R.kz[0] = k0.astype(BF16)
        R.kz[1] = k1.astype(BF16)
        R.kt[0] = k0.T.astype(BF16)
        R.kt[1] = k1.T.astype(BF16)
        q = qkv[:, pl.ds(0, 128)].astype(F32)
        R.vz[0] = jnp.where(keep, q, 0.0).astype(BF16)
        R.vz[1] = jnp.where(keep, 0.0, q).astype(BF16)
        tick(ticks.get(3, ()))
        for c in qc:
            c.wait_recv()
        tick(ticks.get(7, ()))
        g2 = R.dc[...].astype(F32)
        et = (g2 * ctx[...]).T
        R.inner[0:1] = jnp.sum(et[0:64], axis=0, keepdims=True)
        R.inner[1:2] = jnp.sum(et[64:128], axis=0, keepdims=True)
        R.cz[0] = jnp.where(keep, g2, 0.0).astype(BF16)
        R.cz[1] = jnp.where(keep, 0.0, g2).astype(BF16)
        if l == 1:
            reload.append(local(R.sx2, ctx))
        R.et[...] = jnp.zeros_like(R.et)
        base = L.used
        L.used += SQ

        def unrotate(v, co, si):
            return v * co - swap_halves(v) * si

        kv = pl.ds(128, 256)

        def back(p, i):
            return L.describe(i, R.sb.at[p, :, kv], R.rx.at[s, :, kv], (d, p))

        @pl.loop(0, LEN // QB)
        def _(i):
            at = pl.ds(pl.multiple_of(i * QB, QB), QB)
            v = qkv[at, pl.ds(256, 128)]
            vf = v.astype(F32)
            pick = low_lanes((QB, 128))
            dk, dv = None, None
            for j in range(2):
                vz = (jnp.where(pick, vf, 0.0) if j == 0 else jnp.where(pick, 0.0, vf)).astype(BF16)
                pr = jnp.exp(mm_t(R.kz[j, at], qkv[:, pl.ds(0, 128)]) - lse[pl.ds(j, 1)])
                dp = mm_t(vz, R.dc[...])
                ds = (pr * (dp - R.inner[pl.ds(j, 1)])).astype(BF16)
                a = mm(pr.astype(BF16), R.cz[j])
                b = mm(ds, R.vz[j])
                dv = a if dv is None else dv + a
                dk = b if dk is None else dk + b
                R.et[...] += mm(R.kt[j, :, at], ds)
            dk = unrotate(dk, R.cosf[at], R.sinf[at]).astype(BF16)
            dv = dv.astype(BF16)
            for h in range(QB // TOK):
                p = (QB // TOK) * i + h
                R.sb[p, :, pl.ds(128, 128)] = dk[TOK * h : TOK * (h + 1)]
                R.sb[p, :, pl.ds(256, 128)] = dv[TOK * h : TOK * (h + 1)]
                k = lax.rem(p - s + SQ, SQ)

                @pl.when(k != 0)
                def _():
                    back(p, base + k).start()

        dq = unrotate(R.et[...].T * (HEAD**-0.5), R.cosf[...], R.sinf[...])
        for p in range(SQ):
            R.sb[p, :, pl.ds(0, 128)] = dq[TOK * p : TOK * (p + 1)].astype(BF16)
        qs = pl.ds(0, 128)
        bc = [L.copy(R.sb.at[p, :, qs], R.rx.at[s, :, qs], (d, p)) for p in L.seq_peers]
        R.rx[s] = R.sb[s]
        tick(ticks.get(4, ()))
        for c in bc:
            c.wait_recv()
        for k in range(1, SQ):
            c = back(L.seq_peers[k - 1], base + k)
            c.wait_recv()
            c.wait_send()
        tick(ticks.get(5, ()))
        unpack_pairs(R.rx, R.tb)
        for c in (1 - L.x, L.x):
            a = R.tb[chip(c)]
            for t in range(3):
                cs = pl.ds(256 * t, 256)
                part[chip(c), cs] = mm_t(a, wq[cs])
        L.settle()
        c_other = reduce_chip("a", 1)
        c_own = reduce_chip("a", 0)
        c_cross = reduce_cross("a", c_other)
        grad_of("qkv", x, R.tb)
        if l == 1:
            reload.append(local(R.st4, x))
        tick(ticks.get(6, ()))
        R.gres[...] = R.gres[...] + reduce_end("a", c_own, c_cross)
        L.settle()
        for c in reload:
            c.wait()

    L.settle_slow()
    backward(1, TICKS[0])
    lone_end(0, lone_out, R.hres[pl.ds(0, TOK)], R.out)
    backward(0, TICKS[1])
    lone_in = lone_begin(1, R.gres[pl.ds(TOK, PART)])
    vcp = L.copy(R.va, R.vy, L.yp)
    vcp.wait_recv()
    R.vb[...] = R.va[...] + R.vy[...]
    vzc = [L.copy(R.vb, R.vz3.at[k], L.zdev[k]) for k in range(ZS - 1)]
    tick(TICKS[2][0])
    for c in vzc:
        c.wait_recv()
    R.vc[...] = R.vb[...] + R.vz3[0] + R.vz3[1] + R.vz3[2]
    vsc = L.copy(R.vc, R.vs, (L.sib, s))
    lone_end(1, lone_in, R.gres[pl.ds(0, TOK)], R.gin)
    tick(TICKS[2][1])
    vsc.wait_recv()
    R.vd[...] = R.vc[...] + R.vs[...]
    vxc = L.copy(R.vd, R.vx, (L.xp, s))
    tick(TICKS[2][2])
    vxc.wait_recv()
    R.vsum[...] = R.vd[...] + R.vx[...]
    L.settle()
    L.settle_slow()
    for total in sums:
        total.settle()


def of(names, layer):
    return [n + str(layer) for n in names]


def staggered(chunks, beats=40, depth=11):
    return [[c for c, begin in reversed(chunks) if 0 <= t - begin < depth] for t in range(beats)]


FEED = "gGuU"
LATER = of(FEED, 1) + of(FEED, 0)
LAST = staggered(list(zip(of("dgDGuUqro", 0), (0, 0, 0, 1, 1, 2, 2, 3, 3))))
LAST[0] = of("oqr", 1) + LAST[0]
LAST[1] = LAST[1] + of(FEED, 1)
LAST[2] = of("oqr", 1) + LAST[2]
LAST[4] = of("oqr", 1) + LAST[4]
TICKS = [
    {5: of("gGuUdD", 1), 6: of("o", 1)},
    {0: of("dD", 1), 1: of(FEED, 1), 7: of(FEED, 1), 5: of(FEED, 0) + of("gGuUdDoqr", 1), 6: []},
    {0: LAST[0], 1: LAST[1], 2: sum(LAST[2:], []) + of("dDgGuUoqr", 1)},
]


def rotary():
    half = HEAD // 2
    freqs = 1000.0 ** (-(np.arange(half) * 2.0 / HEAD))
    angles = np.arange(LEN)[:, None] * freqs[None, :]
    co, si = np.cos(angles), np.sin(angles)
    table = np.concatenate([co] * 4, axis=1), np.concatenate([-si, si, -si, si], axis=1)
    return [jnp.asarray(t, F32) for t in table]


def shared_device(inputs, cotangent, live, *weights):
    sets = (weights[:9], weights[9:])
    d = lax.axis_index("dp")
    cosf, sinf = rotary()
    norms = jnp.concatenate([jnp.pad(sets[i][j].astype(F32), (0, 64)) for i in range(2) for j in (2, 3, 7, 8)]).reshape(8, 256)
    flags = jnp.broadcast_to(live.astype(F32), (2, 256))
    aux = jnp.concatenate([norms, flags, jnp.zeros((6, 256), F32)], axis=0)
    args = [inputs[:, 0], cotangent[:, 0], aux]
    for i in range(2):
        args += [sets[i][0], sets[i][4], sets[i][5], sets[i][1], sets[i][6]]
    args += [cosf, sinf]
    outs = OUTS + OUTS_ANY
    res = pl.pallas_call(
        whole_kernel,
        name="layers",
        out_shape=[jax.ShapeDtypeStruct(*o) for _, o in outs],
        in_specs=[pl.BlockSpec(memory_space=pl.ANY if n in INS_ANY else pltpu.VMEM) for n in INS],
        out_specs=[pl.BlockSpec(memory_space=pltpu.VMEM)] * len(OUTS) + [pl.BlockSpec(memory_space=pl.ANY)] * len(OUTS_ANY),
        scratch_shapes=[pltpu.VMEM(*o) for _, o in SCRATCH]
        + [
            pltpu.SemaphoreType.DMA((SEMS,)),
            pltpu.SemaphoreType.DMA((SEMS,)),
            pltpu.SemaphoreType.DMA((64,)),
        ],
        cost_estimate=pl.CostEstimate(flops=4 * 10**10, bytes_accessed=5 * 10**7, transcendentals=10**7),
        compiler_params=pltpu.CompilerParams(collective_id=1, has_side_effects=True, vmem_limit_bytes=VMEM_LIMIT),
    )(*args)
    grads = pl.pallas_call(
        widen_kernel,
        name="widen",
        out_shape=[jax.ShapeDtypeStruct(*o) for o in GRADS + GRADS + [((2, TOK, D), BF16)] * 2],
        in_specs=[pl.BlockSpec(memory_space=pl.ANY)] * 4,
        out_specs=[pl.BlockSpec(memory_space=pl.ANY)] * 12,
        scratch_shapes=[
            pltpu.VMEM((2, BLOCKS, QR, D), BF16),
            pltpu.VMEM((STAGES, QR, D), F32),
            pltpu.SemaphoreType.DMA((12,)),
            pltpu.SemaphoreType.DMA((STAGES,)),
        ],
        cost_estimate=pl.CostEstimate(flops=10**7, bytes_accessed=3 * 10**7, transcendentals=0),
        compiler_params=pltpu.CompilerParams(vmem_limit_bytes=40 * 2**20),
    )(res[3], res[4], res[0], res[1])
    vsum = lax.dynamic_slice_in_dim(res[2], d * QR, QR, 1)
    out = [grads[10][:, None], grads[11][:, None]]
    for i in range(2):
        g_qkv, g_out, g_gate, g_up, g_down = grads[5 * i : 5 * i + 5]
        v = vsum[4 * i : 4 * i + 4]
        out += [g_qkv, g_out, v[0], v[1], g_gate, g_up, g_down, v[2], v[3]]
    return tuple(out)


def fits(mesh):
    return mesh.shape["dp"] == DP and mesh.shape["seq"] == SQ


def as_sent(array):
    return jax.tree.map(lambda a: a.astype(jnp.bfloat16) if a.dtype == jnp.float32 else a, array)


def tables(positions):
    half = HEAD // 2
    freqs = 1000.0 ** (-(jnp.arange(half).astype(jnp.float32) * 2.0 / HEAD))
    angles = positions[:, None] * freqs[None, :]
    return (jnp.cos(angles), jnp.sin(angles))


def rotate(values, cosine, sine):
    half = HEAD // 2
    first = values[..., :half]
    second = values[..., half:]
    cos_b = cosine[:, None, :]
    sin_b = sine[:, None, :]
    return jnp.concatenate(
        [first * cos_b - second * sin_b, second * cos_b + first * sin_b], axis=-1
    )


def unrotate(values, cosine, sine):
    half = HEAD // 2
    first = values[..., :half]
    second = values[..., half:]
    cos_b = cosine[:, None, :]
    sin_b = sine[:, None, :]
    return jnp.concatenate(
        [first * cos_b + second * sin_b, second * cos_b - first * sin_b], axis=-1
    )


def layer_norm(rows, gain, shift):
    center = rows - jnp.mean(rows, axis=-1, keepdims=True)
    spread = jnp.mean(center * center, axis=-1, keepdims=True)
    return center * lax.rsqrt(spread + 1e-05) * gain + shift


def dot_first(left, right):
    return lax.dot_general(
        left, right, (((0,), (0,)), ((), ())), preferred_element_type=jnp.float32
    )


def dot_last(left, right):
    return lax.dot_general(
        left, right, (((1,), (1,)), ((), ())), preferred_element_type=jnp.float32
    )


def forward_layer(hidden_in, weights, cosine, sine):
    w_qkv, w_out, gain_a, shift_a, w_gate, w_up, w_down, gain_f, shift_f = weights
    tokens = hidden_in.shape[0]
    width = hidden_in.shape[1]
    heads = width // HEAD
    scale = HEAD ** (-0.5)
    act = hidden_in.astype(jnp.bfloat16)
    joint = jnp.dot(act, w_qkv, preferred_element_type=jnp.float32)
    query = joint[:, :width].reshape(tokens, heads, HEAD)
    keys = joint[:, width : 2 * width].reshape(tokens, heads, HEAD)
    query_r = rotate(query, cosine, sine).astype(jnp.bfloat16)
    keys_r = rotate(keys, cosine, sine).astype(jnp.bfloat16).reshape(tokens, width)
    values_r = joint[:, 2 * width :].astype(jnp.bfloat16)
    keys_all, values_all = (
        lax.all_gather(keys_r, "seq", axis=0, tiled=True),
        lax.all_gather(values_r, "seq", axis=0, tiled=True),
    )
    length = keys_all.shape[0]
    keys_all = keys_all.reshape(length, heads, HEAD)
    values_all = values_all.reshape(length, heads, HEAD)
    scores = (
        jnp.einsum("qhd,khd->hqk", query_r, keys_all, preferred_element_type=jnp.float32) * scale
    )
    top = jnp.max(scores, axis=-1, keepdims=True)
    expo = jnp.exp(scores - top)
    total = jnp.sum(expo, axis=-1, keepdims=True)
    probs = expo / total
    log_total = top + jnp.log(total)
    context = jnp.einsum(
        "hqk,khd->qhd", probs.astype(jnp.bfloat16), values_all, preferred_element_type=jnp.float32
    )
    context = context.reshape(tokens, width).astype(jnp.bfloat16)
    res_a = hidden_in + jnp.dot(context, w_out, preferred_element_type=jnp.float32)
    norm_a = layer_norm(res_a, gain_a.astype(jnp.float32), shift_a.astype(jnp.float32))
    act_f = norm_a.astype(jnp.bfloat16)
    gate_pre = jnp.dot(act_f, w_gate, preferred_element_type=jnp.float32)
    up_pre = jnp.dot(act_f, w_up, preferred_element_type=jnp.float32)
    hidden = (jax.nn.silu(gate_pre) * up_pre).astype(jnp.bfloat16)
    res_f = norm_a + jnp.dot(hidden, w_down, preferred_element_type=jnp.float32)
    result = layer_norm(res_f, gain_f.astype(jnp.float32), shift_f.astype(jnp.float32))
    saved = (
        act,
        query_r,
        keys_r,
        values_r,
        log_total,
        context,
        res_a,
        act_f,
        gate_pre,
        up_pre,
        hidden,
        res_f,
    )
    return (result, saved)


def backward_layer(grad_out, weights, saved, cosine, sine):
    w_qkv, w_out, gain_a, shift_a, w_gate, w_up, w_down, gain_f, shift_f = weights
    (
        act,
        query_r,
        keys_r,
        values_r,
        log_total,
        context,
        res_a,
        act_f,
        gate_pre,
        up_pre,
        hidden,
        res_f,
    ) = saved
    tokens = act.shape[0]
    width = act.shape[1]
    heads = width // HEAD
    scale = HEAD ** (-0.5)
    unused, pull_f = jax.vjp(
        layer_norm, res_f, gain_f.astype(jnp.float32), shift_f.astype(jnp.float32)
    )
    d_res_f, d_gain_f, d_shift_f = pull_f(grad_out)
    d_branch = d_res_f.astype(jnp.bfloat16)
    g_down = dot_first(hidden, d_branch)
    d_hidden = dot_last(d_branch, w_down)
    sigm = jax.nn.sigmoid(gate_pre)
    d_gate = (d_hidden * up_pre * sigm * (1.0 + gate_pre * (1.0 - sigm))).astype(jnp.bfloat16)
    d_up = (d_hidden * gate_pre * sigm).astype(jnp.bfloat16)
    g_gate = dot_first(act_f, d_gate)
    g_up = dot_first(act_f, d_up)
    d_norm_a = d_res_f + dot_last(d_gate, w_gate) + dot_last(d_up, w_up)
    unused, pull_a = jax.vjp(
        layer_norm, res_a, gain_a.astype(jnp.float32), shift_a.astype(jnp.float32)
    )
    d_res_a, d_gain_a, d_shift_a = pull_a(d_norm_a)
    d_attn = d_res_a.astype(jnp.bfloat16)
    g_out = dot_first(context, d_attn)
    d_context = dot_last(d_attn, w_out).astype(jnp.bfloat16).reshape(tokens, heads, HEAD)
    keys_all, values_all = (
        lax.all_gather(keys_r, "seq", axis=0, tiled=True),
        lax.all_gather(values_r, "seq", axis=0, tiled=True),
    )
    length = keys_all.shape[0]
    keys_all = keys_all.reshape(length, heads, HEAD)
    values_all = values_all.reshape(length, heads, HEAD)
    scores = (
        jnp.einsum("qhd,khd->hqk", query_r, keys_all, preferred_element_type=jnp.float32) * scale
    )
    probs = jnp.exp(scores - log_total)
    d_probs = jnp.einsum("qhd,khd->hqk", d_context, values_all, preferred_element_type=jnp.float32)
    inner = jnp.sum(probs * d_probs, axis=-1, keepdims=True)
    d_scores = (probs * (d_probs - inner)).astype(jnp.bfloat16)
    d_query = (
        jnp.einsum("hqk,khd->qhd", d_scores, keys_all, preferred_element_type=jnp.float32) * scale
    )
    d_keys_all = (
        jnp.einsum("hqk,qhd->khd", d_scores, query_r, preferred_element_type=jnp.float32) * scale
    )
    d_values_all = jnp.einsum(
        "hqk,qhd->khd", probs.astype(jnp.bfloat16), d_context, preferred_element_type=jnp.float32
    )
    d_keys, d_values = (
        lax.psum_scatter(
            d_keys_all.reshape(length, width).astype(jnp.bfloat16),
            "seq",
            scatter_dimension=0,
            tiled=True,
        ).astype(jnp.float32),
        lax.psum_scatter(
            d_values_all.reshape(length, width).astype(jnp.bfloat16),
            "seq",
            scatter_dimension=0,
            tiled=True,
        ).astype(jnp.float32),
    )
    d_query = unrotate(d_query, cosine, sine).reshape(tokens, width)
    d_keys = unrotate(d_keys.reshape(tokens, heads, HEAD), cosine, sine).reshape(tokens, width)
    d_joint = jnp.concatenate([d_query, d_keys, d_values], axis=1).astype(jnp.bfloat16)
    g_qkv = dot_first(act, d_joint)
    grad_in = d_res_a + dot_last(d_joint, w_qkv)
    return (grad_in, (g_qkv, g_out, d_gain_a, d_shift_a, g_gate, g_up, g_down, d_gain_f, d_shift_f))


def per_device(
    inputs,
    cotangent,
    live,
    first_qkv,
    first_out,
    first_gain_a,
    first_shift_a,
    first_gate,
    first_up,
    first_down,
    first_gain_f,
    first_shift_f,
    second_qkv,
    second_out,
    second_gain_a,
    second_shift_a,
    second_gate,
    second_up,
    second_down,
    second_gain_f,
    second_shift_f,
):
    local_sets = (
        (
            first_qkv,
            first_out,
            first_gain_a,
            first_shift_a,
            first_gate,
            first_up,
            first_down,
            first_gain_f,
            first_shift_f,
        ),
        (
            second_qkv,
            second_out,
            second_gain_a,
            second_shift_a,
            second_gate,
            second_up,
            second_down,
            second_gain_f,
            second_shift_f,
        ),
    )
    micro = inputs.shape[0]
    tokens = inputs.shape[2]
    groups = lax.axis_size("dp")
    positions = (lax.axis_index("seq") * tokens + jnp.arange(tokens)).astype(jnp.float32)
    cosine, sine = tables(positions)
    totals = [
        tuple(
            (jnp.zeros((w.shape[0] * groups,) + w.shape[1:], jnp.float32) for w in local_sets[0])
        ),
        tuple(
            (jnp.zeros((w.shape[0] * groups,) + w.shape[1:], jnp.float32) for w in local_sets[1])
        ),
    ]
    results = []
    grads_in = []
    for batch in range(micro):
        flag = live[batch, 0].astype(jnp.float32)
        state = inputs[batch, 0].astype(jnp.float32)
        held = []
        saves = []
        for index in range(2):
            full = lax.all_gather(as_sent(local_sets[index]), "dp", axis=0, tiled=True)
            held.append(full)
            state, saved = forward_layer(state, full, cosine, sine)
            saves.append(saved)
        results.append((state * flag).astype(jnp.bfloat16))
        grad = cotangent[batch, 0].astype(jnp.float32) * flag
        for index in (1, 0):
            full = lax.all_gather(as_sent(local_sets[index]), "dp", axis=0, tiled=True)
            grad, terms = backward_layer(grad, full, saves[index], cosine, sine)
            totals[index] = tuple((old + new for old, new in zip(totals[index], terms)))
        grads_in.append(grad.astype(jnp.bfloat16))
    summed = []
    for index in range(2):
        shares = jax.tree.map(
            lambda part: part.astype(jnp.float32),
            lax.psum_scatter(as_sent(totals[index]), "dp", scatter_dimension=0, tiled=True),
        )
        final = jax.tree.map(
            lambda part: part.astype(jnp.float32), lax.psum(as_sent(shares), "seq")
        )
        summed.extend(final)
    output = jnp.stack(results)[:, None]
    input_grad = jnp.stack(grads_in)[:, None]
    return (output, input_grad) + tuple(summed)


def solution(mesh):
    def device(inputs, cotangent, *rest):
        if fits(mesh) and inputs.shape == (2, 1, TOK, D):
            return shared_device(inputs, cotangent, *rest)
        return per_device(inputs, cotangent, *rest)

    return jax.shard_map(
        device,
        mesh=mesh,
        in_specs=(
            P(None, "dp", "seq", None),
            P(None, "dp", "seq", None),
            P(None, "dp"),
            P("dp", None),
            P("dp", None),
            P("dp"),
            P("dp"),
            P("dp", None),
            P("dp", None),
            P("dp", None),
            P("dp"),
            P("dp"),
            P("dp", None),
            P("dp", None),
            P("dp"),
            P("dp"),
            P("dp", None),
            P("dp", None),
            P("dp", None),
            P("dp"),
            P("dp"),
        ),
        out_specs=(
            P(None, "dp", "seq", None),
            P(None, "dp", "seq", None),
            P("dp", None),
            P("dp", None),
            P("dp"),
            P("dp"),
            P("dp", None),
            P("dp", None),
            P("dp", None),
            P("dp"),
            P("dp"),
            P("dp", None),
            P("dp", None),
            P("dp"),
            P("dp"),
            P("dp", None),
            P("dp", None),
            P("dp", None),
            P("dp"),
            P("dp"),
        ),
        check_vma=False,
    )
```
